128 devices in a mesh: ctx: 32 (over z, y, core), ch: 4 (over x).
Axes of the slice: x: 4, y: 4, z: 4, core: 2. Of those that a mesh axis runs over, the one named last changes fastest.
Arguments:
- query: bfloat16 [4096, 4096], P('ctx', 'ch'), may hold values from -6 to 6
- key_in: bfloat16 [4096, 4096], P('ctx', 'ch'), may hold values from -6 to 6
- value_in: bfloat16 [4096, 4096], P('ctx', 'ch'), may hold values from -6 to 6
- filter_raw: bfloat16 [4096, 4096], P(None, 'ch'), may hold values from -2523.4375 to 2523.4375
- decay: float32 [4096], P('ch'), may hold values from 0.0007324219 to 0.0029296875
- skip: float32 [4096], P('ch'), may hold values from -3 to 3
- out_weight: bfloat16 [4096, 4096], P('ch'), may hold values from -0.09375 to 0.09375
- cotangent: bfloat16 [4096, 4096], P('ctx', 'ch'), may hold values from -6 to 6
Outputs:
- mixed: bfloat16 [4096, 4096], P('ctx', 'ch')
- d_query: bfloat16 [4096, 4096], P('ctx', 'ch')
- d_key: bfloat16 [4096, 4096], P('ctx', 'ch')
- d_value: bfloat16 [4096, 4096], P('ctx', 'ch')
- filter_grad: float32 [4096, 4096], P('ctx', 'ch')
- skip_grad: float32 [4096], P('ch')
The draws below stay inside these ranges and needn't reach their ends.
All inputs are finite; a program needn't handle non-finite values.
Results may differ from the reference program's by a relative error of at most 0.013.
Values may be sent and summed in bfloat16 or wider, within the bound.
No kernel may reach another device: no remote copies, remote signals or barrier semaphores. Data moves between devices by JAX's collectives and lax.ppermute only.
A program may use at most 384 MiB of HBM per device.

```python
import math
import jax
import jax.numpy as jnp

CH = 4096
LENGTH = 4096


def decay_rates(key):
    local = jax.random.fold_in(key, 11)
    spread = jax.random.uniform(local, (CH,), jnp.float32)
    rates = jnp.exp(jnp.log(3.0 / LENGTH) + spread * jnp.log(4.0))
    return jnp.clip(rates, 3.0 / LENGTH, 12.0 / LENGTH).astype(jnp.float32)


def draw_decay(key, part):
    rates = decay_rates(key)
    return rates


def draw_filter_raw(key, part):
    rates = decay_rates(key)
    key = jax.random.fold_in(key, 5)
    noise = jnp.clip(jax.random.normal(key, (LENGTH, CH), jnp.float32), -6.0, 6.0)
    lags = jnp.arange(LENGTH, dtype=jnp.float32)
    envelope = jnp.exp(0.85 * rates[None, :] * lags[:, None])
    return (noise * envelope / math.sqrt(LENGTH)).astype(jnp.bfloat16)


def level_of(own_key, extent, split, least, largest):
    loudness, own = 1.0, jax.random.fold_in(own_key, 6)
    for axis_at, blocks in split:
        steps = jnp.exp(jax.random.uniform(jax.random.fold_in(own, axis_at), (blocks,), jnp.float32, least / len(split), largest / len(split)))
        loudness = loudness * jnp.repeat(steps, extent[axis_at] // blocks).reshape([-1 if axis == axis_at else 1 for axis in range(len(extent))])
    return loudness


def gaussian(stream_key, dims, width, bound, cuts=(), kind=jnp.bfloat16):
    loudness = level_of(stream_key, dims, cuts, -0.22, 0.18) if cuts else 1.0
    drawn = jax.random.normal(stream_key, dims, jnp.float32) * width * loudness
    return jnp.minimum(jnp.maximum(drawn, -bound), bound).astype(kind)


def setup_inputs(seed: int = 0) -> dict:
    keys = jax.random.split(jax.random.key(seed), 9)
    query = gaussian(keys[0], (LENGTH, CH), 1.0, 6.0, ((0, 32), (1, 4)))
    key_in = gaussian(keys[1], (LENGTH, CH), 1.0, 6.0, ((0, 32), (1, 4)))
    value_in = gaussian(keys[2], (LENGTH, CH), 1.0, 6.0, ((0, 32), (1, 4)))
    filter_raw = draw_filter_raw(jax.random.fold_in(keys[8], 71), 0)
    decay = draw_decay(jax.random.fold_in(keys[8], 71), 0)
    skip = gaussian(keys[5], (CH,), 0.5, 3.0, ((0, 4),), jnp.float32)
    out_weight = gaussian(keys[6], (CH, CH), CH ** -0.5, 0.09375, ((0, 4),))
    cotangent = gaussian(keys[7], (LENGTH, CH), 1.0, 6.0, ((0, 32), (1, 4)))
    return {"query": query, "key_in": key_in, "value_in": value_in, "filter_raw": filter_raw, "decay": decay, "skip": skip, "out_weight": out_weight, "cotangent": cotangent}


def causal(taps, signal):
    size = 2 * taps.shape[0]
    product = jnp.fft.rfft(taps, n=size, axis=0) * jnp.fft.rfft(signal, n=size, axis=0)
    return jnp.fft.irfft(product, n=size, axis=0)[:taps.shape[0]]


def reference(query, key_in, value_in, filter_raw, decay, skip, out_weight, cotangent):
    key_float = key_in.astype(jnp.float32)
    value_float = value_in.astype(jnp.float32)
    query_float = query.astype(jnp.float32)
    product_in = (key_float * value_float).astype(jnp.bfloat16)
    product_float = product_in.astype(jnp.float32)
    positions = jnp.arange(LENGTH, dtype=jnp.float32)
    window = jnp.exp(-decay[None, :] * positions[:, None])
    taps = filter_raw.astype(jnp.float32) * window
    convolved = causal(taps, product_float) + skip[None, :] * product_float
    gated = (query_float * convolved).astype(jnp.bfloat16)
    mixed = jnp.dot(gated, out_weight, preferred_element_type=jnp.float32).astype(jnp.bfloat16)
    back_grad = jnp.dot(cotangent, out_weight.T, preferred_element_type=jnp.float32)
    conv_grad = (query_float * back_grad).astype(jnp.bfloat16)
    grad_float = conv_grad.astype(jnp.float32)
    d_query = (back_grad * convolved).astype(jnp.bfloat16)
    input_grad = causal(taps, grad_float[::-1])[::-1] + skip[None, :] * grad_float
    d_key = (input_grad * value_float).astype(jnp.bfloat16)
    d_value = (input_grad * key_float).astype(jnp.bfloat16)
    size = 2 * LENGTH
    spectrum = jnp.fft.rfft(grad_float, n=size, axis=0) * jnp.conj(jnp.fft.rfft(product_float, n=size, axis=0))
    correlation = jnp.fft.irfft(spectrum, n=size, axis=0)[:LENGTH]
    filter_grad = correlation * window
    skip_grad = jnp.sum(grad_float * product_float, axis=0)
    return mixed, d_query, d_key, d_value, filter_grad, skip_grad
```

```python
from functools import partial

import jax
import jax.numpy as jnp
import ml_dtypes
import numpy as np
from jax import lax
from jax.experimental import pallas as pl
from jax.experimental.pallas import tpu as pltpu
from jax.sharding import PartitionSpec as P

PANEL = 128
PANELS = 32
OWN = 32
CHB = 1024
ROWS = PANELS * OWN
SPLIT = 4
PAIRS = OWN // 2
TAIL = 16
GROUP = 8
F32 = jnp.float32
BF16 = jnp.bfloat16
LIMIT = 24 * 1024 * 1024


def tables():
    freq = np.arange(PANEL) + 0.5
    spot = np.arange(PANEL)
    angle = 2 * np.pi * spot[:, None] * freq[None, :] / (2 * PANEL)
    inner = np.concatenate([np.cos(angle), -np.sin(angle)], axis=1)
    inner_back = np.concatenate([np.cos(angle.T), -np.sin(angle.T)], axis=0) / (
        PANEL * 2 * PANELS
    )
    turn = 2 * np.pi * np.arange(2 * PANELS)[:, None] * np.arange(PANELS)[None, :] / (2 * PANELS)
    cos, sin = np.cos(turn), np.sin(turn)
    outer = np.concatenate(
        [np.concatenate([cos, sin], axis=1), np.concatenate([-sin, cos], axis=1)], axis=0
    )
    outer_back = np.concatenate(
        [np.concatenate([cos.T, -sin.T], axis=1), np.concatenate([sin.T, cos.T], axis=1)], axis=0
    )
    return [m.astype(ml_dtypes.bfloat16) for m in (inner, outer, outer_back, inner_back)]


def dot(left, right):
    return jnp.dot(left, right, preferred_element_type=F32)


def dot_rows(left, right):
    return lax.dot_general(left, right, (((1,), (1,)), ((), ())), preferred_element_type=F32)


def spectrum(load, inner, outer, mid_ref, store):
    step = 8
    for a in range(0, PANELS, step):
        rows = dot(jnp.concatenate([load(a + b) for b in range(step)], axis=0), inner)
        mid_ref[0, pl.ds(a * OWN, step * OWN), :] = rows[:, :PANEL]
        mid_ref[1, pl.ds(a * OWN, step * OWN), :] = rows[:, PANEL:]
    for pair in range(PAIRS):
        quarter = [
            [mid_ref[part, pl.ds(2 * pair + c, PANELS, stride=OWN), :].astype(BF16) for c in (0, 1)]
            for part in (0, 1)
        ]
        both = jnp.concatenate([jnp.concatenate(q, axis=1) for q in quarter], axis=0)
        store(pair, dot(outer, both))


def spread(pair, freq, outer_back, mid_ref):
    back = dot(outer_back, freq.astype(BF16))
    for part in (0, 1):
        for c in (0, 1):
            mid_ref[part, pl.ds(2 * pair + c, PANELS, stride=OWN), :] = back[
                part * PANELS : (part + 1) * PANELS, c * PANEL : (c + 1) * PANEL
            ]


def gather_panels(mid_ref, inner_back, shift, store):
    lanes = lax.broadcasted_iota(jnp.int32, (1, PANEL), 1)
    sign = (1.0 - 2.0 * (lanes % 2).astype(F32)) * shift
    step = 8
    for a in range(0, PANELS, step):
        parts = []
        for b in range(a, a + step):
            real = mid_ref[0, pl.ds(b * OWN, OWN), :]
            imag = mid_ref[1, pl.ds(b * OWN, OWN), :]
            other = b - shift
            if 0 <= other < PANELS:
                there_real = mid_ref[0, pl.ds(other * OWN, OWN), :]
                there_imag = mid_ref[1, pl.ds(other * OWN, OWN), :]
                real = real - sign * there_imag
                imag = imag + sign * there_real
            parts.append(jnp.concatenate([real.astype(BF16), imag.astype(BF16)], axis=1))
        done = dot(jnp.concatenate(parts, axis=0), inner_back)
        for b in range(step):
            store(a + b, done[b * OWN : (b + 1) * OWN])


def product_kernel(key_ref, value_ref, out_ref, key_held, value_held, sems):
    copies = [
        pltpu.make_async_copy(ref, held, sems.at[n])
        for n, (ref, held) in enumerate(((key_ref, key_held), (value_ref, value_held)))
    ]
    for copy in copies:
        copy.start()
    for copy in copies:
        copy.wait()
    product = key_held[...].astype(F32) * value_held[...].astype(F32)
    out_ref[...] = product.T.astype(BF16).reshape(PANELS, OWN, PANEL)


def filter_kernel(
    where_ref,
    raw_ref,
    decay_ref,
    inner_from,
    outer_from,
    freq_to,
    rate_ref,
    inner_ref,
    outer_ref,
    freq_ref,
    raw_held,
    decay_held,
    taps_ref,
    mid_ref,
    sems,
):
    column = pl.multiple_of(lax.div(where_ref[0], SPLIT) * PANEL, PANEL)
    moves = (
        (raw_ref.at[:, pl.ds(column, PANEL)], raw_held),
        (decay_ref, decay_held),
        (inner_from, inner_ref),
        (outer_from, outer_ref),
    )
    copies = [pltpu.make_async_copy(here, there, sems.at[n]) for n, (here, there) in enumerate(moves)]
    for copy in copies:
        copy.start()
    for copy in copies:
        copy.wait()
    place = lax.rem(where_ref[0], SPLIT) * OWN
    row = lax.broadcasted_iota(jnp.int32, (OWN, PANEL), 0)
    lane = lax.broadcasted_iota(jnp.int32, (OWN, PANEL), 1)
    mine = lane == row + place
    rates = decay_held[pl.ds(lax.div(where_ref[0], SPLIT), 1), :]
    rate = jnp.sum(jnp.where(mine, rates, 0.0), axis=1, keepdims=True)
    rate = jnp.broadcast_to(rate, (OWN, PANEL))
    rate_ref[...] = rate
    choose = mine.astype(BF16)
    step = 4
    for a in range(0, PANELS, step):
        chosen = dot_rows(choose, raw_held[pl.ds(a * PANEL, step * PANEL), :])
        for b in range(step):
            spot = (lane + (a + b) * PANEL).astype(F32)
            taps = chosen[:, b * PANEL : (b + 1) * PANEL] * jnp.exp(-rate * spot)
            taps_ref[a + b] = taps.astype(BF16)

    group = 4
    writes = []

    def store(pair, value):
        freq_ref[pair] = value
        if (pair + 1) % group == 0:
            part = pl.ds(pair + 1 - group, group)
            copy = pltpu.make_async_copy(
                freq_ref.at[part], freq_to.at[part], sems.at[4 + pair // group]
            )
            copy.start()
            writes.append(copy)

    spectrum(lambda a: taps_ref[a], inner_ref[...], outer_ref[...], mid_ref, store)
    for copy in writes:
        copy.wait()


def halves(value):
    return value[: 2 * PANELS], value[2 * PANELS :]


def forward_kernel(
    where_ref,
    x_ref,
    filter_from,
    inner_ref,
    outer_ref,
    outer_back_from,
    inner_back_from,
    query_ref,
    cot0_ref,
    cot1_ref,
    cot2_ref,
    cot3_ref,
    weight_ref,
    send_ref,
    freq_ref,
    back_ref,
    grad_ref,
    mid_ref,
    out_mid_ref,
    outer_back_ref,
    inner_back_ref,
    filter_ref,
    cot_held,
    weight_held,
    sems,
):
    moves = [
        (outer_back_from, outer_back_ref),
        (inner_back_from, inner_back_ref),
        (filter_from, filter_ref),
    ]
    for s, cot_ref in enumerate((cot0_ref, cot1_ref, cot2_ref, cot3_ref)):
        block = lax.rem(where_ref[1] + SPLIT - s, SPLIT)
        columns = pl.ds(pl.multiple_of(block * CHB, CHB), CHB)
        moves += [(cot_ref, cot_held.at[s]), (weight_ref.at[:, columns], weight_held.at[s])]
    copies = [pltpu.make_async_copy(there, to, sems.at[n]) for n, (there, to) in enumerate(moves)]
    for copy in copies:
        copy.start()

    def store(pair, value):
        freq_ref[pair] = value

    spectrum(lambda a: x_ref[a], inner_ref[...], outer_ref[...], mid_ref, store)
    for copy in copies[:3]:
        copy.wait()
    outer_back = outer_back_ref[...]
    for pair in range(PAIRS):
        xr, xi = halves(freq_ref[pair])
        hr, hi = halves(filter_ref[pair])
        spread(
            pair,
            jnp.concatenate([hr * xr - hi * xi, hr * xi + hi * xr], axis=0),
            outer_back,
            out_mid_ref,
        )

    def store_panel(a, value):
        send_ref[a, :OWN, :] = value.astype(BF16)

    gather_panels(out_mid_ref, inner_back_ref[...], 1, store_panel)
    for copy in copies[3:]:
        copy.wait()
    chunk = 256
    for c in range(0, CHB, chunk):
        total = jnp.zeros((PANEL, chunk), F32)
        for s in range(SPLIT):
            total += dot_rows(cot_held[s], weight_held[s, pl.ds(c, chunk), :])
        back_ref[:, pl.ds(c, chunk)] = total
        grad = query_ref[:, pl.ds(c, chunk)].astype(F32) * total
        grad_ref[:, pl.ds(c, chunk)] = grad.astype(BF16)
        turned = grad.T.astype(BF16)
        for b in range(chunk // OWN):
            send_ref[c // OWN + b, OWN:, :] = turned[b * OWN : (b + 1) * OWN]


def middle_kernel(
    where_ref,
    got_ref,
    x_ref,
    freq_ref,
    rate_ref,
    inner_ref,
    outer_ref,
    query_ref,
    key_ref,
    value_ref,
    skip_ref,
    back_ref,
    filter_from,
    outer_back_from,
    inner_back_from,
    weight_from,
    own_to,
    one_to,
    two_to,
    three_to,
    send_to,
    d_query_ref,
    outer_back_ref,
    inner_back_ref,
    filter_ref,
    weight_ref,
    spec_ref,
    mid_ref,
    lag_mid_ref,
    in_mid_ref,
    gated_ref,
    own_ref,
    part_ref,
    send_ref,
    sems,
):
    order = (2, 1, 3, 0)
    moves = [
        (outer_back_from, outer_back_ref),
        (inner_back_from, inner_back_ref),
        (filter_from, filter_ref),
    ]
    for s in order:
        block = lax.rem(where_ref[1] + s, SPLIT)
        columns = pl.ds(pl.multiple_of(block * CHB, CHB), CHB)
        moves.append((weight_from.at[:, columns], weight_ref.at[s]))
    loads = [pltpu.make_async_copy(there, to, sems.at[n]) for n, (there, to) in enumerate(moves)]
    for copy in loads:
        copy.start()
    writes = []

    def write(there, to):
        copy = pltpu.make_async_copy(there, to, sems.at[len(loads) + len(writes)])
        copy.start()
        writes.append(copy)

    def store(pair, value):
        spec_ref[pair] = value

    spectrum(lambda a: got_ref[a, OWN:, :], inner_ref[...], outer_ref[...], mid_ref, store)
    for copy in loads[:3]:
        copy.wait()
    outer_back = outer_back_ref[...]
    for pair in range(PAIRS):
        gr, gi = halves(spec_ref[pair])
        for other_ref, out_ref in ((filter_ref, in_mid_ref), (freq_ref, lag_mid_ref)):
            hr, hi = halves(other_ref[pair])
            spread(
                pair,
                jnp.concatenate([gr * hr + gi * hi, gi * hr - gr * hi], axis=0),
                outer_back,
                out_ref,
            )

    chunk = 256
    for c in range(0, CHB, chunk):
        at = pl.ds(c, chunk)
        turned = got_ref[pl.ds(c // OWN, chunk // OWN), :OWN, :].reshape(chunk, PANEL).astype(F32).T
        product = (key_ref[:, at].astype(F32) * value_ref[:, at].astype(F32)).astype(BF16)
        convolved = turned + skip_ref[:, at] * product.astype(F32)
        gated_ref[:, at] = (query_ref[:, at].astype(F32) * convolved).astype(BF16)
        d_query_ref[:, at] = (back_ref[:, at] * convolved).astype(BF16)
    outs = (own_to, one_to, two_to, three_to)
    for n, s in enumerate(order):
        loads[3 + n].wait()
        for c in range(0, CHB, chunk):
            part = dot(gated_ref[...], weight_ref[s, :, pl.ds(c, chunk)])
            if s:
                part_ref[s - 1, :, pl.ds(c, chunk)] = part.astype(BF16)
            else:
                own_ref[:, pl.ds(c, chunk)] = part
        write(part_ref.at[s - 1] if s else own_ref, outs[s])

    def store_input(a, value):
        send_ref[a, :OWN, :] = value.astype(BF16)

    gather_panels(in_mid_ref, inner_back_ref[...], -1, store_input)
    rate = rate_ref[...]
    lane = lax.broadcasted_iota(jnp.int32, (OWN, PANEL), 1)
    sums = jnp.zeros((OWN, PANEL), F32)
    for a in range(PANELS):
        sums += got_ref[a, OWN:, :].astype(F32) * x_ref[a].astype(F32)
    total = jnp.sum(sums, axis=1, keepdims=True)
    place = lax.rem(where_ref[0], SPLIT) * OWN
    row = lax.broadcasted_iota(jnp.int32, (OWN, PANEL), 0)
    line = jnp.sum(jnp.where(lane == row + place, total, 0.0), axis=0, keepdims=True)
    high = line.astype(BF16).astype(F32)
    low = line - high
    index = lax.broadcasted_iota(jnp.int32, (TAIL, PANEL), 0)
    tail = jnp.where(index == 0, high, jnp.where(index == 1, low, 0.0)).astype(BF16)
    for a in range(PANELS):
        send_ref[a, 2 * OWN :, :] = tail

    def store_lag(a, value):
        window = jnp.exp(-rate * (lane + a * PANEL).astype(F32))
        send_ref[a, OWN : 2 * OWN, :] = (value * window).astype(BF16)
        if (a + 1) % GROUP == 0:
            part = pl.ds(a + 1 - GROUP, GROUP)
            write(send_ref.at[part], send_to.at[part])

    gather_panels(lag_mid_ref, inner_back_ref[...], -1, store_lag)
    for copy in writes:
        copy.wait()


def mixed_kernel(own_from, one_ref, two_ref, three_ref, mixed_ref, own_ref, sem):
    copy = pltpu.make_async_copy(own_from, own_ref, sem)
    copy.start()
    copy.wait()
    chunk = 256
    for c in range(0, CHB, chunk):
        at = pl.ds(c, chunk)
        mixed = own_ref[:, at] + one_ref[:, at].astype(F32)
        mixed += two_ref[:, at].astype(F32) + three_ref[:, at].astype(F32)
        mixed_ref[:, at] = mixed.astype(BF16)


def finish_kernel(
    got_ref,
    key_ref,
    value_ref,
    grad_ref,
    skip_ref,
    d_key_ref,
    d_value_ref,
    lag_ref,
    skip_grad_ref,
):
    chunk = 256
    for c in range(0, CHB, chunk):
        at = pl.ds(c, chunk)
        block = pl.ds(c // OWN, chunk // OWN)
        lag_ref[:, at] = got_ref[block, OWN : 2 * OWN, :].reshape(chunk, PANEL).astype(F32).T
        turned = got_ref[block, :OWN, :].reshape(chunk, PANEL).astype(F32).T
        grad = turned + skip_ref[:, at] * grad_ref[:, at].astype(F32)
        d_key_ref[:, at] = (grad * value_ref[:, at].astype(F32)).astype(BF16)
        d_value_ref[:, at] = (grad * key_ref[:, at].astype(F32)).astype(BF16)
    for r in range(PANELS // SPLIT):
        line = jnp.zeros((1, PANEL), F32)
        for b in range(SPLIT):
            tail = got_ref[r * SPLIT + b, 2 * OWN :, :].astype(F32)
            line += tail[0:1] + tail[1:2]
        skip_grad_ref[pl.ds(r, 1), :] = line


VMEM = pl.BlockSpec(memory_space=pltpu.VMEM)
SMEM = pl.BlockSpec(memory_space=pltpu.SMEM)
HBM = pl.BlockSpec(memory_space=pltpu.HBM)
ANY = pl.BlockSpec(memory_space=pl.ANY)
FREQ = (PAIRS, 4 * PANELS, 2 * PANEL)
MID = pltpu.VMEM((2, ROWS, PANEL), F32)
BLOCK = (PANEL, CHB)


def shape(dims, kind):
    return jax.ShapeDtypeStruct(dims, kind)


def here(dims, kind):
    return pltpu.VMEM(dims, kind)


def far(dims, kind):
    return pltpu.HBM(dims, kind)


def call(kernel, in_specs, out_shape, scratch, flops, name, out_specs=None):
    run = pl.pallas_call(
        kernel,
        in_specs=in_specs,
        out_specs=out_specs or jax.tree.map(lambda _: VMEM, out_shape),
        out_shape=out_shape,
        scratch_shapes=scratch,
        compiler_params=pltpu.CompilerParams(vmem_limit_bytes=LIMIT),
        cost_estimate=pl.CostEstimate(flops=flops, bytes_accessed=1 << 20, transcendentals=0),
        name=name,
    )

    def bound(*args):
        return run(
            *(
                pltpu.with_memory_space_constraint(arg, pltpu.HBM) if spec is HBM else arg
                for arg, spec in zip(args, in_specs, strict=True)
            )
        )

    return bound


def make_product(key_in, value_in):
    scratch = [pltpu.VMEM(BLOCK, BF16), pltpu.VMEM(BLOCK, BF16), pltpu.SemaphoreType.DMA((2,))]
    return call(
        product_kernel, [HBM] * 2, shape((PANELS, OWN, PANEL), BF16), scratch, 1 << 20, "product"
    )(key_in, value_in)


def make_filter(where, filter_raw, decay, inner, outer):
    out = [far(FREQ, F32), here((OWN, PANEL), F32)]
    out += [here(m.shape, BF16) for m in (inner, outer)]
    scratch = [
        pltpu.VMEM(FREQ, F32),
        pltpu.VMEM((PANELS * PANEL, PANEL), BF16),
        pltpu.VMEM(decay.shape, F32),
        pltpu.VMEM((PANELS, OWN, PANEL), BF16),
        MID,
        pltpu.SemaphoreType.DMA((8,)),
    ]
    specs = [SMEM] + [HBM] * 4
    return call(filter_kernel, specs, out, scratch, 1 << 32, "taps", [HBM] + [VMEM] * 3)(
        where, filter_raw, decay, inner, outer
    )


def make_forward(where, x, freq_filter, mats, query, cots, weight):
    out = [
        shape((PANELS, 2 * OWN, PANEL), BF16),
        here(FREQ, F32),
        here(BLOCK, F32),
        here(BLOCK, BF16),
    ]
    scratch = [
        MID,
        MID,
        pltpu.VMEM(mats[2].shape, BF16),
        pltpu.VMEM(mats[3].shape, BF16),
        pltpu.VMEM(FREQ, F32),
        pltpu.VMEM((SPLIT, *BLOCK), BF16),
        pltpu.VMEM((SPLIT, CHB, CHB), BF16),
        pltpu.SemaphoreType.DMA((3 + 2 * SPLIT,)),
    ]
    specs = [SMEM, VMEM, HBM, VMEM, VMEM] + [HBM] * 2 + [VMEM, HBM] + [ANY] * 3 + [HBM]
    return call(
        forward_kernel, specs, out, scratch, 1 << 33, "forward"
    )(where, x, freq_filter, *mats, query, *cots, weight)


def make_middle(where, got, x, freq_x, rate, held, query, key_in, value_in, skip, back, *rest):
    dims = (PANELS, 2 * OWN + TAIL, PANEL)
    out = [far(BLOCK, F32)] + [far(BLOCK, BF16)] * 3 + [far(dims, BF16), shape(BLOCK, BF16)]
    scratch = [
        pltpu.VMEM(rest[1].shape, BF16),
        pltpu.VMEM(rest[2].shape, BF16),
        pltpu.VMEM(FREQ, F32),
        pltpu.VMEM((SPLIT, CHB, CHB), BF16),
        pltpu.VMEM(FREQ, F32),
        MID,
        MID,
        MID,
        pltpu.VMEM(BLOCK, BF16),
        pltpu.VMEM(BLOCK, F32),
        pltpu.VMEM((SPLIT - 1, *BLOCK), BF16),
        pltpu.VMEM(dims, BF16),
        pltpu.SemaphoreType.DMA((3 + 2 * SPLIT + PANELS // GROUP,)),
    ]
    return call(
        middle_kernel,
        [SMEM] + [VMEM] * 11 + [HBM] * 4,
        out,
        scratch,
        1 << 33,
        "middle",
        [HBM] * 5 + [VMEM],
    )(where, got, x, freq_x, rate, *held, query, key_in, value_in, skip, back, *rest)


def make_mixed(parts):
    scratch = [pltpu.VMEM(BLOCK, F32), pltpu.SemaphoreType.DMA]
    specs = [HBM] + [VMEM] * 3
    return call(mixed_kernel, specs, shape(BLOCK, BF16), scratch, 1 << 36, "mixed")(*parts)


def make_finish(got, key_in, value_in, grad, skip):
    out = [shape(BLOCK, BF16)] * 2 + [shape(BLOCK, F32), shape((CHB // PANEL, PANEL), F32)]
    return call(finish_kernel, [VMEM] * 5, out, [], 1 << 20, "finish")(
        got, key_in, value_in, grad, skip
    )


def shifted(value, step):
    return lax.ppermute(value, "ch", [(i, (i + step) % SPLIT) for i in range(SPLIT)])


def exchange(value):
    return lax.all_to_all(value, "ctx", 0, 0)


def local(query, key_in, value_in, filter_raw, decay, skip, out_weight, cotangent):
    mats = [jnp.asarray(m) for m in tables()]
    where = jnp.stack([lax.axis_index("ctx"), lax.axis_index("ch")]).astype(jnp.int32)
    cots = [cotangent] + [shifted(cotangent, s) for s in (1, 2, 3)]
    x = exchange(make_product(key_in, value_in))
    freq_filter, rate, *held = make_filter(
        where, filter_raw, decay.reshape(CHB // PANEL, PANEL), *mats[:2]
    )
    send, freq_x, back, grad = make_forward(
        where, x, freq_filter, held + mats[2:], query, cots, out_weight
    )
    got = exchange(send)
    skip_row = skip.reshape(1, CHB)
    rest = (freq_filter, *mats[2:], out_weight)
    own, one, two, three, last, d_query = make_middle(
        where, got, x, freq_x, rate, held, query, key_in, value_in, skip_row, back, *rest
    )
    last = exchange(last)
    mixed = make_mixed([own, shifted(one, 1), shifted(two, 2), shifted(three, 3)])
    d_key, d_value, filter_grad, skip_grad = make_finish(last, key_in, value_in, grad, skip_row)
    return (mixed, d_query, d_key, d_value, filter_grad, skip_grad.reshape(CHB))


def solution(mesh):
    in_specs = (
        P("ctx", "ch"),
        P("ctx", "ch"),
        P("ctx", "ch"),
        P(None, "ch"),
        P("ch"),
        P("ch"),
        P("ch", None),
        P("ctx", "ch"),
    )
    out_specs = (
        P("ctx", "ch"),
        P("ctx", "ch"),
        P("ctx", "ch"),
        P("ctx", "ch"),
        P("ctx", "ch"),
        P("ch"),
    )
    return jax.shard_map(local, mesh=mesh, in_specs=in_specs, out_specs=out_specs, check_vma=False)
```

```python
from functools import partial

import jax
import jax.numpy as jnp
import ml_dtypes
import numpy as np
from jax import lax
from jax.experimental import pallas as pl
from jax.experimental.pallas import tpu as pltpu
from jax.sharding import PartitionSpec as P

PANEL = 128
PANELS = 32
TURNS = 2 * PANELS
OWN = 32
PITCH = 40
CHB = 1024
SPLIT = 4
CHUNK = 256
GROUP = 8
TAIL = 16
F32 = jnp.float32
BF16 = jnp.bfloat16
LIMIT = 24 * 1024 * 1024


def tables():
    freq = np.arange(PANEL) + 0.5
    angle = 2 * np.pi * np.arange(PANEL)[:, None] * freq[None, :] / (2 * PANEL)
    turn = 2 * np.pi * np.arange(TURNS)[:, None] * np.arange(PANELS)[None, :] / TURNS
    cos, sin = np.cos(angle), np.sin(angle)
    inner = np.block([[cos, -sin], [sin, cos]])
    inner_back = np.concatenate([cos.T, -sin.T], axis=0) / (PANEL * TURNS)
    cos, sin = np.cos(turn), np.sin(turn)
    outer = np.concatenate([cos, -sin], axis=0)
    outer_back = np.block([[cos.T, -sin.T], [sin.T, cos.T]])
    return [m.astype(ml_dtypes.bfloat16) for m in (outer, inner, outer_back, inner_back)]


def dot(left, right):
    return jnp.dot(left, right, preferred_element_type=F32)


def dot_rows(left, right):
    return lax.dot_general(left, right, (((1,), (1,)), ((), ())), preferred_element_type=F32)


def spectrum(mid_ref, outer, inner, store):
    for c in range(0, OWN, 4):
        rows = []
        for b in (c, c + 2):
            pair = [mid_ref[0, pl.ds(b + q, PANELS, stride=PITCH), :].astype(BF16) for q in (0, 1)]
            both = dot(outer, jnp.concatenate(pair, axis=1)).astype(BF16)
            for q in (0, 1):
                one = both[:, q * PANEL : (q + 1) * PANEL]
                rows.append(jnp.concatenate([one[:TURNS], one[TURNS:]], axis=1))
        store(c, dot(jnp.concatenate(rows, axis=0), inner).astype(BF16))


def rows_of(freq_ref, c):
    both = freq_ref[pl.ds(c * TURNS, TURNS), :].astype(F32)
    return both[:, :PANEL], both[:, PANEL:]


def spread(c, columns, outer_back, mid_ref):
    back = dot(outer_back, jnp.concatenate(columns, axis=1))
    for part in (0, 1):
        for q in range(len(columns)):
            mid_ref[part, pl.ds(c + q, PANELS, stride=PITCH), :] = back[
                part * PANELS : (part + 1) * PANELS, q * PANEL : (q + 1) * PANEL
            ]


def gather_panels(mid_ref, inner_back, shift, store):
    lanes = lax.broadcasted_iota(jnp.int32, (1, PANEL), 1)
    sign = (1.0 - 2.0 * (lanes % 2).astype(F32)) * shift
    for a in range(0, PANELS, GROUP):
        parts = []
        for b in range(a, a + GROUP):
            real = mid_ref[0, pl.ds(b * PITCH, OWN), :]
            imag = mid_ref[1, pl.ds(b * PITCH, OWN), :]
            other = b - shift
            if 0 <= other < PANELS:
                there_real = mid_ref[0, pl.ds(other * PITCH, OWN), :]
                there_imag = mid_ref[1, pl.ds(other * PITCH, OWN), :]
                real = real - sign * there_imag
                imag = imag + sign * there_real
            parts.append(jnp.concatenate([real.astype(BF16), imag.astype(BF16)], axis=1))
        done = dot(jnp.concatenate(parts, axis=0), inner_back)
        for b in range(GROUP):
            store(a + b, done[b * OWN : (b + 1) * OWN])


def start_all(moves, sems, first=0):
    copies = [pltpu.make_async_copy(here, to, sems.at[first + n]) for n, (here, to) in enumerate(moves)]
    for copy in copies:
        copy.start()
    return copies


def wait_all(copies):
    for copy in copies:
        copy.wait()


def product_kernel(key_from, value_from, out_ref, key_ref, value_ref, sems):
    wait_all(start_all([(key_from, key_ref), (value_from, value_ref)], sems))
    product = key_ref[...].astype(F32) * value_ref[...].astype(F32)
    out_ref[...] = product.T.astype(BF16).reshape(PANELS, OWN, PANEL)


def filter_kernel(
    where_ref,
    raw_from,
    decay_from,
    skip_from,
    outer_from,
    inner_from,
    query_from,
    freq_to,
    rate_ref,
    own_skip_ref,
    outer_ref,
    inner_ref,
    turned_ref,
    freq_ref,
    raw_ref,
    decay_ref,
    skip_ref,
    query_ref,
    mid_ref,
    sems,
):
    column = pl.ds(pl.multiple_of(lax.div(where_ref[0], SPLIT) * PANEL, PANEL), PANEL)
    moves = [(decay_from, decay_ref)]
    for n in range(SPLIT):
        rows = pl.ds(n * CHB, CHB)
        moves.append((raw_from.at[rows, column], raw_ref.at[rows, :]))
    moves += [(outer_from, outer_ref), (inner_from, inner_ref), (skip_from, skip_ref)]
    moves.append((query_from, query_ref))
    loads = start_all(moves, sems)
    place = lax.rem(where_ref[0], SPLIT) * OWN
    row = lax.broadcasted_iota(jnp.int32, (OWN, PANEL), 0)
    lane = lax.broadcasted_iota(jnp.int32, (OWN, PANEL), 1)
    mine = lane == row + place
    choose = mine.astype(BF16)
    loads[0].wait()

    def own_column(ref):
        line = ref[pl.ds(lax.div(where_ref[0], SPLIT), 1), :]
        column = jnp.sum(jnp.where(mine, line, 0.0), axis=1, keepdims=True)
        return jnp.broadcast_to(column, (OWN, PANEL))

    rate = own_column(decay_ref)
    rate_ref[...] = rate
    for n in range(SPLIT):
        loads[1 + n].wait()
        for a in range(n * GROUP, (n + 1) * GROUP, 4):
            chosen = dot_rows(choose, raw_ref[pl.ds(a * PANEL, 4 * PANEL), :])
            for b in range(4):
                spot = (lane + (a + b) * PANEL).astype(F32)
                taps = chosen[:, b * PANEL : (b + 1) * PANEL] * jnp.exp(-rate * spot)
                mid_ref[0, pl.ds((a + b) * PITCH, OWN), :] = taps
    wait_all(loads[1 + SPLIT :])
    own_skip_ref[...] = own_column(skip_ref)
    for c in range(0, CHB, CHUNK):
        at = pl.ds(c, CHUNK)
        turned_ref[at, :] = query_ref[:, at].astype(F32).T.astype(BF16)
    writes = []

    def store(c, rows):
        part = pl.ds(c * TURNS, 4 * TURNS)
        freq_ref[part, :] = rows
        writes.extend(start_all([(freq_ref.at[part], freq_to.at[part])], sems, len(moves) + len(writes)))

    spectrum(mid_ref, outer_ref[...], inner_ref[...], store)
    wait_all(writes)


def forward_kernel(
    where_ref,
    x_ref,
    own_skip_ref,
    outer_ref,
    inner_ref,
    query_ref,
    cot1_ref,
    cot2_ref,
    cot3_ref,
    cot0_ref,
    filter_from,
    outer_back_from,
    inner_back_from,
    weight_from,
    send_ref,
    freq_ref,
    back_ref,
    mid_ref,
    outer_back_ref,
    inner_back_ref,
    filter_ref,
    cot_ref,
    weight_ref,
    sems,
):
    moves = [
        (outer_back_from, outer_back_ref),
        (inner_back_from, inner_back_ref),
        (filter_from, filter_ref),
    ]
    moves += [(ref, cot_ref.at[s]) for s, ref in enumerate((cot0_ref, cot1_ref, cot2_ref, cot3_ref))]
    loads = start_all(moves, sems)

    def weight_copy(n):
        rows = pl.ds(pl.multiple_of(n * CHUNK, CHUNK), CHUNK)
        return pltpu.make_async_copy(
            weight_from.at[rows, :], weight_ref.at[rows, :], sems.at[len(moves) + n]
        )

    for n in range(CHB // CHUNK):
        weight_copy(n).start()
    for a in range(PANELS):
        mid_ref[0, pl.ds(a * PITCH, OWN), :] = x_ref[a].astype(F32)

    def store(c, rows):
        freq_ref[pl.ds(c * TURNS, 4 * TURNS), :] = rows

    spectrum(mid_ref, outer_ref[...], inner_ref[...], store)
    wait_all(loads[:3])
    outer_back = outer_back_ref[...]
    for c in range(0, OWN, 2):
        columns = []
        for b in (c, c + 1):
            xr, xi = rows_of(freq_ref, b)
            hr, hi = rows_of(filter_ref, b)
            columns.append(
                jnp.concatenate(
                    [(hr * xr - hi * xi).astype(BF16), (hr * xi + hi * xr).astype(BF16)], axis=0
                )
            )
        spread(c, columns, outer_back, mid_ref)

    own_skip = own_skip_ref[...]

    def store_panel(a, value):
        send_ref[a, :OWN, :] = (value + own_skip * x_ref[a].astype(F32)).astype(BF16)

    gather_panels(mid_ref, inner_back_ref[...], 1, store_panel)
    wait_all(loads[3:])
    starts = [lax.rem(where_ref[1] + SPLIT - s, SPLIT) * CHB for s in range(SPLIT)]
    columns = [pl.ds(pl.multiple_of(start, CHB), CHB) for start in starts]

    @pl.loop(0, CHB // CHUNK)
    def _(n):
        weight_copy(n).wait()
        at = pl.ds(pl.multiple_of(n * CHUNK, CHUNK), CHUNK)
        total = dot_rows(weight_ref[at, columns[0]], cot_ref[0])
        for s in range(1, SPLIT):
            total += dot_rows(weight_ref[at, columns[s]], cot_ref[s])
        back_ref[at, :] = total
        grad = (query_ref[at, :].astype(F32) * total).astype(BF16)
        for b in range(CHUNK // OWN):
            send_ref[n * (CHUNK // OWN) + b, OWN:, :] = grad[b * OWN : (b + 1) * OWN]


def middle_kernel(
    where_ref,
    got_ref,
    x_ref,
    freq_ref,
    rate_ref,
    own_skip_ref,
    outer_ref,
    inner_ref,
    query_ref,
    back_ref,
    filter_from,
    outer_back_from,
    inner_back_from,
    weight_from,
    own_to,
    one_to,
    two_to,
    three_to,
    send_to,
    d_query_to,
    outer_back_ref,
    inner_back_ref,
    filter_ref,
    spec_ref,
    mid_ref,
    lag_ref,
    gated_ref,
    d_query_ref,
    part_ref,
    send_ref,
    weight_ref,
    sems,
):
    moves = [
        (outer_back_from, outer_back_ref),
        (inner_back_from, inner_back_ref),
        (filter_from, filter_ref),
    ]
    loads = start_all(moves, sems)
    writes = []

    def write(this, to):
        writes.extend(start_all([(this, to)], sems, len(moves) + SPLIT + len(writes)))

    def weight_copy(n, s):
        block = lax.rem(where_ref[1] + s, SPLIT) * CHB
        columns = pl.ds(pl.multiple_of(block, CHB), CHB)
        return pltpu.make_async_copy(
            weight_from.at[:, columns], weight_ref.at[n], sems.at[len(moves) + n]
        )

    for n, s in enumerate((2, 1, 3, 0)):
        weight_copy(n, s).start()
    for c in range(0, CHB, CHUNK):
        at = pl.ds(c, CHUNK)
        block = got_ref[pl.ds(c // OWN, CHUNK // OWN), :OWN, :].reshape(CHUNK, PANEL)
        convolved = block.astype(F32)
        gated_ref[:, at] = (query_ref[at, :].astype(F32) * convolved).T.astype(BF16)
        d_query_ref[:, at] = (back_ref[at, :] * convolved).T.astype(BF16)
    write(d_query_ref, d_query_to)
    for a in range(PANELS):
        mid_ref[0, pl.ds(a * PITCH, OWN), :] = got_ref[a, OWN:, :].astype(F32)

    def store(c, rows):
        spec_ref[pl.ds(c * TURNS, 4 * TURNS), :] = rows

    spectrum(mid_ref, outer_ref[...], inner_ref[...], store)
    wait_all(loads)
    outer_back = outer_back_ref[...]
    for c in range(0, OWN, 2):
        columns = {0: [], 1: []}
        for b in (c, c + 1):
            gr, gi = rows_of(spec_ref, b)
            for n, other_ref in enumerate((filter_ref, freq_ref)):
                hr, hi = rows_of(other_ref, b)
                columns[n].append(
                    jnp.concatenate(
                        [(gr * hr + gi * hi).astype(BF16), (gi * hr - gr * hi).astype(BF16)], axis=0
                    )
                )
        spread(c, columns[0], outer_back, mid_ref)
        spread(c, columns[1], outer_back, lag_ref)
    own_skip = own_skip_ref[...]
    sums = [jnp.zeros((OWN, PANEL), F32)]

    def store_input(a, value):
        grad = got_ref[a, OWN:, :].astype(F32)
        sums[0] += grad * x_ref[a].astype(F32)
        send_ref[a, :OWN, :] = (value + own_skip * grad).astype(BF16)

    gather_panels(mid_ref, inner_back_ref[...], -1, store_input)
    rate = rate_ref[...]
    lane = lax.broadcasted_iota(jnp.int32, (OWN, PANEL), 1)
    row = lax.broadcasted_iota(jnp.int32, (OWN, PANEL), 0)
    total = jnp.sum(sums[0], axis=1, keepdims=True)
    place = lax.rem(where_ref[0], SPLIT) * OWN
    line = jnp.sum(jnp.where(lane == row + place, total, 0.0), axis=0, keepdims=True)
    high = line.astype(BF16).astype(F32)
    index = lax.broadcasted_iota(jnp.int32, (TAIL, PANEL), 0)
    tail = jnp.where(index == 0, high, jnp.where(index == 1, line - high, 0.0)).astype(BF16)

    def store_lag(a, value):
        window = jnp.exp(-rate * (lane + a * PANEL).astype(F32))
        send_ref[a, OWN : 2 * OWN, :] = (value * window).astype(BF16)
        send_ref[a, 2 * OWN :, :] = tail
        if (a + 1) % GROUP == 0:
            part = pl.ds(a + 1 - GROUP, GROUP)
            write(send_ref.at[part], send_to.at[part])

    gather_panels(lag_ref, inner_back_ref[...], -1, store_lag)
    outs = (two_to, one_to, three_to, own_to)
    base = len(moves) + SPLIT + len(writes)
    writes += [
        pltpu.make_async_copy(part_ref.at[n], to, sems.at[base + n]) for n, to in enumerate(outs)
    ]

    @pl.loop(0, SPLIT)
    def _(n):
        weight_copy(n, 0).wait()
        for c in range(0, CHB, CHUNK):
            at = pl.ds(c, CHUNK)
            part_ref[n, :, at] = dot(gated_ref[...], weight_ref[n, :, at]).astype(BF16)
        for k in range(SPLIT):

            @pl.when(n == k)
            def _():
                writes[k - SPLIT].start()

    wait_all(writes)


def mixed_kernel(own_from, one_ref, two_ref, three_ref, mixed_ref, own_ref, sem):
    copy = pltpu.make_async_copy(own_from, own_ref, sem)
    copy.start()
    copy.wait()
    for c in range(0, CHB, CHUNK):
        at = pl.ds(c, CHUNK)
        mixed = own_ref[:, at].astype(F32) + one_ref[:, at].astype(F32)
        mixed += two_ref[:, at].astype(F32) + three_ref[:, at].astype(F32)
        mixed_ref[:, at] = mixed.astype(BF16)


def finish_kernel(got_ref, key_ref, value_ref, d_key_ref, d_value_ref, lag_ref, skip_grad_ref):
    for c in range(0, CHB, CHUNK):
        at = pl.ds(c, CHUNK)
        block = pl.ds(c // OWN, CHUNK // OWN)
        lag_ref[:, at] = got_ref[block, OWN : 2 * OWN, :].reshape(CHUNK, PANEL).astype(F32).T
        grad = got_ref[block, :OWN, :].reshape(CHUNK, PANEL).astype(F32).T
        d_key_ref[:, at] = (grad * value_ref[:, at].astype(F32)).astype(BF16)
        d_value_ref[:, at] = (grad * key_ref[:, at].astype(F32)).astype(BF16)
    for r in range(PANELS // SPLIT):
        line = jnp.zeros((1, PANEL), F32)
        for b in range(SPLIT):
            tail = got_ref[r * SPLIT + b, 2 * OWN :, :].astype(F32)
            line += tail[0:1] + tail[1:2]
        skip_grad_ref[pl.ds(r, 1), :] = line


VMEM = pl.BlockSpec(memory_space=pltpu.VMEM)
SMEM = pl.BlockSpec(memory_space=pltpu.SMEM)
HBM = pl.BlockSpec(memory_space=pltpu.HBM)
ANY = pl.BlockSpec(memory_space=pl.ANY)
NEAR = pl.BlockSpec(memory_space=pltpu.VMEM)
FREQ = (OWN * TURNS, 2 * PANEL)
MID = pltpu.VMEM((2, PANELS * PITCH, PANEL), F32)
BLOCK = (PANEL, CHB)
SENT = (PANELS, 2 * OWN, PANEL)
LAST = (PANELS, 2 * OWN + TAIL, PANEL)


def shape(dims, kind):
    return jax.ShapeDtypeStruct(dims, kind)


def here(dims, kind):
    return pltpu.VMEM(dims, kind)


def far(dims, kind):
    return pltpu.HBM(dims, kind)


def call(kernel, in_specs, out_shape, scratch, flops, name, out_specs=None):
    run = pl.pallas_call(
        kernel,
        in_specs=in_specs,
        out_specs=out_specs or jax.tree.map(lambda _: VMEM, out_shape),
        out_shape=out_shape,
        scratch_shapes=scratch,
        compiler_params=pltpu.CompilerParams(vmem_limit_bytes=LIMIT),
        cost_estimate=pl.CostEstimate(flops=flops, bytes_accessed=1 << 20, transcendentals=0),
        name=name,
    )

    def placed(arg, spec):
        if spec is HBM:
            return pltpu.with_memory_space_constraint(arg, pltpu.HBM)
        if spec is NEAR:
            return pltpu.with_memory_space_constraint(arg, pltpu.VMEM)
        return arg

    def bound(*args):
        return run(*(placed(arg, spec) for arg, spec in zip(args, in_specs, strict=True)))

    return bound


def sems(count):
    return pltpu.SemaphoreType.DMA((count,))


def make_product(key_in, value_in):
    scratch = [pltpu.VMEM(BLOCK, BF16), pltpu.VMEM(BLOCK, BF16), sems(2)]
    out = shape((PANELS, OWN, PANEL), BF16)
    return call(product_kernel, [HBM] * 2, out, scratch, 1 << 20, "product")(key_in, value_in)


def make_filter(where, filter_raw, decay, skip, outer, inner, query):
    out = [far(FREQ, BF16), here((OWN, PANEL), F32), here((OWN, PANEL), F32)]
    out += [here(m.shape, BF16) for m in (outer, inner)] + [here((CHB, PANEL), BF16)]
    scratch = [
        pltpu.VMEM(FREQ, BF16),
        pltpu.VMEM((PANELS * PANEL, PANEL), BF16),
        pltpu.VMEM(decay.shape, F32),
        pltpu.VMEM(skip.shape, F32),
        pltpu.VMEM(BLOCK, BF16),
        MID,
        sems(5 + SPLIT + OWN // 4),
    ]
    specs = [SMEM] + [HBM] * 6
    return call(filter_kernel, specs, out, scratch, 1 << 32, "taps", [HBM] + [VMEM] * 5)(
        where, filter_raw, decay, skip, outer, inner, query
    )


def make_forward(where, x, own_skip, held, query, weight, cots, freq_filter, back_mats):
    out = [shape(SENT, BF16), here(FREQ, BF16), here((CHB, PANEL), F32)]
    scratch = [MID] + [pltpu.VMEM(m.shape, BF16) for m in back_mats]
    scratch += [pltpu.VMEM(FREQ, BF16), pltpu.VMEM((SPLIT, *BLOCK), BF16)]
    scratch += [pltpu.VMEM(weight.shape, BF16), sems(3 + SPLIT + CHB // CHUNK)]
    specs = [SMEM] + [VMEM] * 5 + [ANY] * 3 + [HBM] * 5
    return call(forward_kernel, specs, out, scratch, 1 << 33, "forward")(
        where, x, own_skip, *held, query, *cots[1:], cots[0], freq_filter, *back_mats, weight
    )


def make_middle(where, got, x, freq_x, rate, own_skip, held, query, back, *rest):
    out = [far(BLOCK, BF16)] * 4 + [far(LAST, BF16), far(BLOCK, BF16)]
    scratch = [pltpu.VMEM(m.shape, BF16) for m in rest[1:3]]
    scratch += [pltpu.VMEM(FREQ, BF16), pltpu.VMEM(FREQ, BF16), MID, MID]
    scratch += [pltpu.VMEM(BLOCK, BF16)] * 2
    scratch += [pltpu.VMEM((SPLIT, *BLOCK), BF16), pltpu.VMEM(LAST, BF16)]
    scratch += [pltpu.VMEM((SPLIT, CHB, CHB), BF16), sems(4 + 2 * SPLIT + PANELS // GROUP)]
    specs = [SMEM] + [VMEM] * 9 + [HBM] * 4
    return call(middle_kernel, specs, out, scratch, 1 << 33, "middle", [HBM] * 6)(
        where, got, x, freq_x, rate, own_skip, *held, query, back, *rest
    )


def make_mixed(parts):
    scratch = [pltpu.VMEM(BLOCK, BF16), pltpu.SemaphoreType.DMA]
    specs = [HBM] + [VMEM] * 3
    return call(mixed_kernel, specs, shape(BLOCK, BF16), scratch, 1 << 36, "mixed")(*parts)


def make_finish(got, key_in, value_in):
    out = [shape(BLOCK, BF16)] * 2 + [shape(BLOCK, F32), shape((CHB // PANEL, PANEL), F32)]
    return call(finish_kernel, [VMEM] * 3, out, [], 1 << 20, "finish")(got, key_in, value_in)


def shifted(value, step):
    return lax.ppermute(value, "ch", [(i, (i + step) % SPLIT) for i in range(SPLIT)])


def exchange(value):
    return lax.all_to_all(value, "ctx", 0, 0)


def local(query, key_in, value_in, filter_raw, decay, skip, out_weight, cotangent):
    mats = [jnp.asarray(m) for m in tables()]
    where = jnp.stack([lax.axis_index("ctx"), lax.axis_index("ch")]).astype(jnp.int32)
    lines = (CHB // PANEL, PANEL)
    cots = [cotangent] + [shifted(cotangent, s) for s in (1, 2, 3)]
    x = exchange(make_product(key_in, value_in))
    freq_filter, rate, own_skip, *held, turned = make_filter(
        where, filter_raw, decay.reshape(lines), skip.reshape(lines), *mats[:2], query
    )
    send, freq_x, back = make_forward(
        where, x, own_skip, held, turned, out_weight, cots, freq_filter, mats[2:]
    )
    got = exchange(send)
    own, one, two, three, last, d_query = make_middle(
        where, got, x, freq_x, rate, own_skip, held, turned, back, freq_filter, *mats[2:], out_weight
    )
    last = exchange(last)
    mixed = make_mixed([own, shifted(one, 1), shifted(two, 2), shifted(three, 3)])
    d_key, d_value, filter_grad, skip_grad = make_finish(last, key_in, value_in)
    return (mixed, d_query, d_key, d_value, filter_grad, skip_grad.reshape(CHB))


def solution(mesh):
    in_specs = (
        P("ctx", "ch"),
        P("ctx", "ch"),
        P("ctx", "ch"),
        P(None, "ch"),
        P("ch"),
        P("ch"),
        P("ch", None),
        P("ctx", "ch"),
    )
    out_specs = (
        P("ctx", "ch"),
        P("ctx", "ch"),
        P("ctx", "ch"),
        P("ctx", "ch"),
        P("ctx", "ch"),
        P("ch"),
    )
    return jax.shard_map(local, mesh=mesh, in_specs=in_specs, out_specs=out_specs, check_vma=False)
```

```python
from functools import partial

import jax
import jax.numpy as jnp
import ml_dtypes
import numpy as np
from jax import lax
from jax.experimental import pallas as pl
from jax.experimental.pallas import tpu as pltpu
from jax.sharding import PartitionSpec as P

PANEL = 128
PANELS = 32
TURNS = 2 * PANELS
OWN = 32
PITCH = 40
CHB = 1024
SPLIT = 4
CHUNK = 256
GROUP = 8
TAIL = 16
F32 = jnp.float32
BF16 = jnp.bfloat16
LIMIT = 24 * 1024 * 1024


def tables():
    freq = np.arange(PANEL) + 0.5
    angle = 2 * np.pi * np.arange(PANEL)[:, None] * freq[None, :] / (2 * PANEL)
    turn = 2 * np.pi * np.arange(TURNS)[:, None] * np.arange(PANELS)[None, :] / TURNS
    cos, sin = np.cos(angle), np.sin(angle)
    inner = np.block([[cos, -sin], [sin, cos]])
    inner_back = np.concatenate([cos.T, -sin.T], axis=0) / (PANEL * TURNS)
    cos, sin = np.cos(turn), np.sin(turn)
    outer = np.concatenate([cos, -sin], axis=0)
    outer_back = np.block([[cos.T, -sin.T], [sin.T, cos.T]])
    return [m.astype(ml_dtypes.bfloat16) for m in (outer, inner, outer_back, inner_back)]


def dot(left, right):
    return jnp.dot(left, right, preferred_element_type=F32)


def dot_rows(left, right):
    return lax.dot_general(left, right, (((1,), (1,)), ((), ())), preferred_element_type=F32)


def spectrum(mid_ref, outer, inner, store):
    for c in range(0, OWN, 4):
        rows = []
        for b in (c, c + 2):
            pair = [mid_ref[0, pl.ds(b + q, PANELS, stride=PITCH), :].astype(BF16) for q in (0, 1)]
            both = dot(outer, jnp.concatenate(pair, axis=1)).astype(BF16)
            for q in (0, 1):
                one = both[:, q * PANEL : (q + 1) * PANEL]
                rows.append(jnp.concatenate([one[:TURNS], one[TURNS:]], axis=1))
        store(c, dot(jnp.concatenate(rows, axis=0), inner).astype(BF16))


def rows_of(freq_ref, c):
    both = freq_ref[pl.ds(c * TURNS, TURNS), :].astype(F32)
    return both[:, :PANEL], both[:, PANEL:]


def spread(c, columns, outer_back, mid_ref):
    back = dot(outer_back, jnp.concatenate(columns, axis=1))
    for part in (0, 1):
        for q in range(len(columns)):
            mid_ref[part, pl.ds(c + q, PANELS, stride=PITCH), :] = back[
                part * PANELS : (part + 1) * PANELS, q * PANEL : (q + 1) * PANEL
            ]


def gather_panels(mid_ref, inner_back, shift, store):
    lanes = lax.broadcasted_iota(jnp.int32, (1, PANEL), 1)
    sign = (1.0 - 2.0 * (lanes % 2).astype(F32)) * shift
    for a in range(0, PANELS, GROUP):
        parts = []
        for b in range(a, a + GROUP):
            real = mid_ref[0, pl.ds(b * PITCH, OWN), :]
            imag = mid_ref[1, pl.ds(b * PITCH, OWN), :]
            other = b - shift
            if 0 <= other < PANELS:
                there_real = mid_ref[0, pl.ds(other * PITCH, OWN), :]
                there_imag = mid_ref[1, pl.ds(other * PITCH, OWN), :]
                real = real - sign * there_imag
                imag = imag + sign * there_real
            parts.append(jnp.concatenate([real.astype(BF16), imag.astype(BF16)], axis=1))
        done = dot(jnp.concatenate(parts, axis=0), inner_back)
        for b in range(GROUP):
            store(a + b, done[b * OWN : (b + 1) * OWN])


def start_all(moves, sems, first=0):
    copies = [pltpu.make_async_copy(here, to, sems.at[first + n]) for n, (here, to) in enumerate(moves)]
    for copy in copies:
        copy.start()
    return copies


def wait_all(copies):
    for copy in copies:
        copy.wait()


def product_kernel(key_from, value_from, out_ref, key_ref, value_ref, sems):
    wait_all(start_all([(key_from, key_ref), (value_from, value_ref)], sems))
    product = key_ref[...].astype(F32) * value_ref[...].astype(F32)
    out_ref[...] = product.T.astype(BF16).reshape(PANELS, OWN, PANEL)


def filter_kernel(
    where_ref,
    raw_from,
    decay_from,
    skip_from,
    outer_from,
    inner_from,
    query_from,
    cot_from,
    weight_from,
    freq_to,
    rate_ref,
    own_skip_ref,
    outer_ref,
    inner_ref,
    turned_ref,
    share_to,
    freq_ref,
    raw_ref,
    decay_ref,
    skip_ref,
    query_ref,
    cot_ref,
    keep_ref,
    share_ref,
    mid_ref,
    sems,
):
    column = pl.ds(pl.multiple_of(lax.div(where_ref[0], SPLIT) * PANEL, PANEL), PANEL)
    moves = [(decay_from, decay_ref)]
    for n in range(SPLIT):
        rows = pl.ds(n * CHB, CHB)
        moves.append((raw_from.at[rows, column], raw_ref.at[rows, :]))
    moves += [(outer_from, outer_ref), (inner_from, inner_ref), (skip_from, skip_ref)]
    own = pl.ds(pl.multiple_of(where_ref[1] * CHB, CHB), CHB)
    moves += [(query_from, query_ref), (cot_from, cot_ref), (weight_from.at[:, own], keep_ref)]
    loads = start_all(moves, sems)
    place = lax.rem(where_ref[0], SPLIT) * OWN
    row = lax.broadcasted_iota(jnp.int32, (OWN, PANEL), 0)
    lane = lax.broadcasted_iota(jnp.int32, (OWN, PANEL), 1)
    mine = lane == row + place
    choose = mine.astype(BF16)
    loads[0].wait()

    def own_column(ref):
        line = ref[pl.ds(lax.div(where_ref[0], SPLIT), 1), :]
        column = jnp.sum(jnp.where(mine, line, 0.0), axis=1, keepdims=True)
        return jnp.broadcast_to(column, (OWN, PANEL))

    rate = own_column(decay_ref)
    rate_ref[...] = rate
    for n in range(SPLIT):
        loads[1 + n].wait()
        for a in range(n * GROUP, (n + 1) * GROUP, 4):
            chosen = dot_rows(choose, raw_ref[pl.ds(a * PANEL, 4 * PANEL), :])
            for b in range(4):
                spot = (lane + (a + b) * PANEL).astype(F32)
                taps = chosen[:, b * PANEL : (b + 1) * PANEL] * jnp.exp(-rate * spot)
                mid_ref[0, pl.ds((a + b) * PITCH, OWN), :] = taps
    wait_all(loads[1 + SPLIT : -2])
    own_skip_ref[...] = own_column(skip_ref)
    for c in range(0, CHB, CHUNK):
        at = pl.ds(c, CHUNK)
        turned_ref[at, :] = query_ref[:, at].astype(F32).T.astype(BF16)
    wait_all(loads[-2:])
    for c in range(0, CHB, CHUNK):
        at = pl.ds(c, CHUNK)
        share_ref[at, :] = dot_rows(keep_ref[at, :], cot_ref[...])
    writes = start_all([(share_ref, share_to)], sems, len(moves))

    def store(c, rows):
        part = pl.ds(c * TURNS, 4 * TURNS)
        freq_ref[part, :] = rows
        writes.extend(start_all([(freq_ref.at[part], freq_to.at[part])], sems, len(moves) + len(writes)))

    spectrum(mid_ref, outer_ref[...], inner_ref[...], store)
    wait_all(writes)


def forward_kernel(
    where_ref,
    x_ref,
    own_skip_ref,
    outer_ref,
    inner_ref,
    query_ref,
    cot1_ref,
    cot2_ref,
    cot3_ref,
    share_from,
    filter_from,
    outer_back_from,
    inner_back_from,
    weight_from,
    send_ref,
    freq_ref,
    back_ref,
    mid_ref,
    outer_back_ref,
    inner_back_ref,
    filter_ref,
    cot_ref,
    share_ref,
    weight_ref,
    sems,
):
    moves = [
        (outer_back_from, outer_back_ref),
        (inner_back_from, inner_back_ref),
        (filter_from, filter_ref),
    ]
    moves += [(ref, cot_ref.at[s]) for s, ref in enumerate((cot1_ref, cot2_ref, cot3_ref))]
    moves.append((share_from, share_ref))
    loads = start_all(moves, sems)

    def weight_copies(n):
        rows = pl.ds(pl.multiple_of(n * CHUNK, CHUNK), CHUNK)
        copies = []
        for s in range(1, SPLIT):
            block = lax.rem(where_ref[1] + SPLIT - s, SPLIT) * CHB
            columns = pl.ds(pl.multiple_of(block, CHB), CHB)
            sem = sems.at[len(moves) + (SPLIT - 1) * n + s - 1]
            copies.append(
                pltpu.make_async_copy(weight_from.at[rows, columns], weight_ref.at[s - 1, rows, :], sem)
            )
        return copies

    for n in range(CHB // CHUNK):
        for copy in weight_copies(n):
            copy.start()
    for a in range(PANELS):
        mid_ref[0, pl.ds(a * PITCH, OWN), :] = x_ref[a].astype(F32)

    def store(c, rows):
        freq_ref[pl.ds(c * TURNS, 4 * TURNS), :] = rows

    spectrum(mid_ref, outer_ref[...], inner_ref[...], store)
    wait_all(loads[:3])
    outer_back = outer_back_ref[...]
    for c in range(0, OWN, 2):
        columns = []
        for b in (c, c + 1):
            xr, xi = rows_of(freq_ref, b)
            hr, hi = rows_of(filter_ref, b)
            columns.append(
                jnp.concatenate(
                    [(hr * xr - hi * xi).astype(BF16), (hr * xi + hi * xr).astype(BF16)], axis=0
                )
            )
        spread(c, columns, outer_back, mid_ref)

    own_skip = own_skip_ref[...]

    def store_panel(a, value):
        send_ref[a, :OWN, :] = (value + own_skip * x_ref[a].astype(F32)).astype(BF16)

    gather_panels(mid_ref, inner_back_ref[...], 1, store_panel)
    wait_all(loads[3:])

    @pl.loop(0, CHB // CHUNK)
    def _(n):
        wait_all(weight_copies(n))
        at = pl.ds(pl.multiple_of(n * CHUNK, CHUNK), CHUNK)
        total = share_ref[at, :]
        for s in range(SPLIT - 1):
            total += dot_rows(weight_ref[s, at, :], cot_ref[s])
        back_ref[at, :] = total
        grad = (query_ref[at, :].astype(F32) * total).astype(BF16)
        for b in range(CHUNK // OWN):
            send_ref[n * (CHUNK // OWN) + b, OWN:, :] = grad[b * OWN : (b + 1) * OWN]


def middle_kernel(
    where_ref,
    got_ref,
    x_ref,
    freq_ref,
    rate_ref,
    own_skip_ref,
    outer_ref,
    inner_ref,
    query_ref,
    back_ref,
    filter_from,
    outer_back_from,
    inner_back_from,
    weight_from,
    own_to,
    one_to,
    two_to,
    three_to,
    send_to,
    d_query_to,
    outer_back_ref,
    inner_back_ref,
    filter_ref,
    spec_ref,
    mid_ref,
    lag_ref,
    gated_ref,
    d_query_ref,
    part_ref,
    send_ref,
    weight_ref,
    sems,
):
    moves = [
        (outer_back_from, outer_back_ref),
        (inner_back_from, inner_back_ref),
        (filter_from, filter_ref),
    ]
    loads = start_all(moves, sems)
    writes = []

    def write(this, to):
        writes.extend(start_all([(this, to)], sems, len(moves) + SPLIT + len(writes)))

    def weight_copy(n, s):
        block = lax.rem(where_ref[1] + s, SPLIT) * CHB
        columns = pl.ds(pl.multiple_of(block, CHB), CHB)
        return pltpu.make_async_copy(
            weight_from.at[:, columns], weight_ref.at[n], sems.at[len(moves) + n]
        )

    for n, s in enumerate((2, 1, 3, 0)):
        weight_copy(n, s).start()
    for c in range(0, CHB, CHUNK):
        at = pl.ds(c, CHUNK)
        block = got_ref[pl.ds(c // OWN, CHUNK // OWN), :OWN, :].reshape(CHUNK, PANEL)
        convolved = block.astype(F32)
        gated_ref[:, at] = (query_ref[at, :].astype(F32) * convolved).T.astype(BF16)
        d_query_ref[:, at] = (back_ref[at, :] * convolved).T.astype(BF16)
    write(d_query_ref, d_query_to)
    for a in range(PANELS):
        mid_ref[0, pl.ds(a * PITCH, OWN), :] = got_ref[a, OWN:, :].astype(F32)

    def store(c, rows):
        spec_ref[pl.ds(c * TURNS, 4 * TURNS), :] = rows

    spectrum(mid_ref, outer_ref[...], inner_ref[...], store)
    wait_all(loads)
    outer_back = outer_back_ref[...]
    for c in range(0, OWN, 2):
        columns = {0: [], 1: []}
        for b in (c, c + 1):
            gr, gi = rows_of(spec_ref, b)
            for n, other_ref in enumerate((filter_ref, freq_ref)):
                hr, hi = rows_of(other_ref, b)
                columns[n].append(
                    jnp.concatenate(
                        [(gr * hr + gi * hi).astype(BF16), (gi * hr - gr * hi).astype(BF16)], axis=0
                    )
                )
        spread(c, columns[0], outer_back, mid_ref)
        spread(c, columns[1], outer_back, lag_ref)
    own_skip = own_skip_ref[...]
    sums = [jnp.zeros((OWN, PANEL), F32)]

    def store_input(a, value):
        grad = got_ref[a, OWN:, :].astype(F32)
        sums[0] += grad * x_ref[a].astype(F32)
        send_ref[a, :OWN, :] = (value + own_skip * grad).astype(BF16)

    gather_panels(mid_ref, inner_back_ref[...], -1, store_input)
    rate = rate_ref[...]
    lane = lax.broadcasted_iota(jnp.int32, (OWN, PANEL), 1)
    row = lax.broadcasted_iota(jnp.int32, (OWN, PANEL), 0)
    total = jnp.sum(sums[0], axis=1, keepdims=True)
    place = lax.rem(where_ref[0], SPLIT) * OWN
    line = jnp.sum(jnp.where(lane == row + place, total, 0.0), axis=0, keepdims=True)
    high = line.astype(BF16).astype(F32)
    index = lax.broadcasted_iota(jnp.int32, (TAIL, PANEL), 0)
    tail = jnp.where(index == 0, high, jnp.where(index == 1, line - high, 0.0)).astype(BF16)

    def store_lag(a, value):
        window = jnp.exp(-rate * (lane + a * PANEL).astype(F32))
        send_ref[a, OWN : 2 * OWN, :] = (value * window).astype(BF16)
        send_ref[a, 2 * OWN :, :] = tail
        if (a + 1) % GROUP == 0:
            part = pl.ds(a + 1 - GROUP, GROUP)
            write(send_ref.at[part], send_to.at[part])

    gather_panels(lag_ref, inner_back_ref[...], -1, store_lag)
    outs = (two_to, one_to, three_to, own_to)
    base = len(moves) + SPLIT + len(writes)
    writes += [
        pltpu.make_async_copy(part_ref.at[n], to, sems.at[base + n]) for n, to in enumerate(outs)
    ]

    @pl.loop(0, SPLIT)
    def _(n):
        weight_copy(n, 0).wait()
        for c in range(0, CHB, CHUNK):
            at = pl.ds(c, CHUNK)
            part_ref[n, :, at] = dot(gated_ref[...], weight_ref[n, :, at]).astype(BF16)
        for k in range(SPLIT):

            @pl.when(n == k)
            def _():
                writes[k - SPLIT].start()

    wait_all(writes)


def mixed_kernel(own_from, one_ref, two_ref, three_ref, mixed_ref, own_ref, sem):
    copy = pltpu.make_async_copy(own_from, own_ref, sem)
    copy.start()
    copy.wait()
    for c in range(0, CHB, CHUNK):
        at = pl.ds(c, CHUNK)
        mixed = own_ref[:, at].astype(F32) + one_ref[:, at].astype(F32)
        mixed += two_ref[:, at].astype(F32) + three_ref[:, at].astype(F32)
        mixed_ref[:, at] = mixed.astype(BF16)


def finish_kernel(got_ref, key_ref, value_ref, d_key_ref, d_value_ref, lag_ref, skip_grad_ref):
    for c in range(0, CHB, CHUNK):
        at = pl.ds(c, CHUNK)
        block = pl.ds(c // OWN, CHUNK // OWN)
        lag_ref[:, at] = got_ref[block, OWN : 2 * OWN, :].reshape(CHUNK, PANEL).astype(F32).T
        grad = got_ref[block, :OWN, :].reshape(CHUNK, PANEL).astype(F32).T
        d_key_ref[:, at] = (grad * value_ref[:, at].astype(F32)).astype(BF16)
        d_value_ref[:, at] = (grad * key_ref[:, at].astype(F32)).astype(BF16)
    for r in range(PANELS // SPLIT):
        line = jnp.zeros((1, PANEL), F32)
        for b in range(SPLIT):
            tail = got_ref[r * SPLIT + b, 2 * OWN :, :].astype(F32)
            line += tail[0:1] + tail[1:2]
        skip_grad_ref[pl.ds(r, 1), :] = line


VMEM = pl.BlockSpec(memory_space=pltpu.VMEM)
SMEM = pl.BlockSpec(memory_space=pltpu.SMEM)
HBM = pl.BlockSpec(memory_space=pltpu.HBM)
ANY = pl.BlockSpec(memory_space=pl.ANY)
NEAR = pl.BlockSpec(memory_space=pltpu.VMEM)
FREQ = (OWN * TURNS, 2 * PANEL)
MID = pltpu.VMEM((2, PANELS * PITCH, PANEL), F32)
BLOCK = (PANEL, CHB)
SENT = (PANELS, 2 * OWN, PANEL)
LAST = (PANELS, 2 * OWN + TAIL, PANEL)


def shape(dims, kind):
    return jax.ShapeDtypeStruct(dims, kind)


def here(dims, kind):
    return pltpu.VMEM(dims, kind)


def far(dims, kind):
    return pltpu.HBM(dims, kind)


def call(kernel, in_specs, out_shape, scratch, flops, name, out_specs=None):
    run = pl.pallas_call(
        kernel,
        in_specs=in_specs,
        out_specs=out_specs or jax.tree.map(lambda _: VMEM, out_shape),
        out_shape=out_shape,
        scratch_shapes=scratch,
        compiler_params=pltpu.CompilerParams(vmem_limit_bytes=LIMIT),
        cost_estimate=pl.CostEstimate(flops=flops, bytes_accessed=1 << 20, transcendentals=0),
        name=name,
    )

    def placed(arg, spec):
        if spec is HBM:
            return pltpu.with_memory_space_constraint(arg, pltpu.HBM)
        if spec is NEAR:
            return pltpu.with_memory_space_constraint(arg, pltpu.VMEM)
        return arg

    def bound(*args):
        return run(*(placed(arg, spec) for arg, spec in zip(args, in_specs, strict=True)))

    return bound


def sems(count):
    return pltpu.SemaphoreType.DMA((count,))


def make_product(key_in, value_in):
    scratch = [pltpu.VMEM(BLOCK, BF16), pltpu.VMEM(BLOCK, BF16), sems(2)]
    out = shape((PANELS, OWN, PANEL), BF16)
    return call(product_kernel, [HBM] * 2, out, scratch, 1 << 20, "product")(key_in, value_in)


def make_filter(where, filter_raw, decay, skip, outer, inner, query, cot, weight):
    out = [far(FREQ, BF16), here((OWN, PANEL), F32), here((OWN, PANEL), F32)]
    out += [here(m.shape, BF16) for m in (outer, inner)] + [here((CHB, PANEL), BF16)]
    out.append(far((CHB, PANEL), F32))
    scratch = [
        pltpu.VMEM(FREQ, BF16),
        pltpu.VMEM((PANELS * PANEL, PANEL), BF16),
        pltpu.VMEM(decay.shape, F32),
        pltpu.VMEM(skip.shape, F32),
        pltpu.VMEM(BLOCK, BF16),
        pltpu.VMEM(BLOCK, BF16),
        pltpu.VMEM((CHB, CHB), BF16),
        pltpu.VMEM((CHB, PANEL), F32),
        MID,
        sems(8 + SPLIT + OWN // 4),
    ]
    specs = [SMEM] + [HBM] * 8
    return call(filter_kernel, specs, out, scratch, 1 << 32, "taps", [HBM] + [VMEM] * 5 + [HBM])(
        where, filter_raw, decay, skip, outer, inner, query, cot, weight
    )


def make_forward(where, x, own_skip, held, query, share, weight, cots, freq_filter, back_mats):
    out = [shape(SENT, BF16), here(FREQ, BF16), here((CHB, PANEL), F32)]
    scratch = [MID] + [pltpu.VMEM(m.shape, BF16) for m in back_mats]
    scratch += [pltpu.VMEM(FREQ, BF16), pltpu.VMEM((SPLIT - 1, *BLOCK), BF16)]
    scratch += [pltpu.VMEM((CHB, PANEL), F32), pltpu.VMEM((SPLIT - 1, CHB, CHB), BF16)]
    scratch.append(sems(4 + (SPLIT - 1) * (1 + CHB // CHUNK)))
    specs = [SMEM] + [VMEM] * 5 + [ANY] * 3 + [HBM] * 5
    return call(forward_kernel, specs, out, scratch, 1 << 33, "forward")(
        where, x, own_skip, *held, query, *cots, share, freq_filter, *back_mats, weight
    )


def make_middle(where, got, x, freq_x, rate, own_skip, held, query, back, *rest):
    out = [far(BLOCK, BF16)] * 4 + [far(LAST, BF16), far(BLOCK, BF16)]
    scratch = [pltpu.VMEM(m.shape, BF16) for m in rest[1:3]]
    scratch += [pltpu.VMEM(FREQ, BF16), pltpu.VMEM(FREQ, BF16), MID, MID]
    scratch += [pltpu.VMEM(BLOCK, BF16)] * 2
    scratch += [pltpu.VMEM((SPLIT, *BLOCK), BF16), pltpu.VMEM(LAST, BF16)]
    scratch += [pltpu.VMEM((SPLIT, CHB, CHB), BF16), sems(4 + 2 * SPLIT + PANELS // GROUP)]
    specs = [SMEM] + [VMEM] * 9 + [HBM] * 4
    return call(middle_kernel, specs, out, scratch, 1 << 33, "middle", [HBM] * 6)(
        where, got, x, freq_x, rate, own_skip, *held, query, back, *rest
    )


def make_mixed(parts):
    scratch = [pltpu.VMEM(BLOCK, BF16), pltpu.SemaphoreType.DMA]
    specs = [HBM] + [VMEM] * 3
    return call(mixed_kernel, specs, shape(BLOCK, BF16), scratch, 1 << 36, "mixed")(*parts)


def make_finish(got, key_in, value_in):
    out = [shape(BLOCK, BF16)] * 2 + [shape(BLOCK, F32), shape((CHB // PANEL, PANEL), F32)]
    return call(finish_kernel, [VMEM] * 3, out, [], 1 << 20, "finish")(got, key_in, value_in)


def shifted(value, step):
    return lax.ppermute(value, "ch", [(i, (i + step) % SPLIT) for i in range(SPLIT)])


def exchange(value):
    return lax.all_to_all(value, "ctx", 0, 0)


def local(query, key_in, value_in, filter_raw, decay, skip, out_weight, cotangent):
    mats = [jnp.asarray(m) for m in tables()]
    where = jnp.stack([lax.axis_index("ctx"), lax.axis_index("ch")]).astype(jnp.int32)
    lines = (CHB // PANEL, PANEL)
    cots = [shifted(cotangent, s) for s in (1, 2, 3)]
    x = exchange(make_product(key_in, value_in))
    lined = (decay.reshape(lines), skip.reshape(lines))
    freq_filter, rate, own_skip, *held, turned, share = make_filter(
        where, filter_raw, *lined, *mats[:2], query, cotangent, out_weight
    )
    send, freq_x, back = make_forward(
        where, x, own_skip, held, turned, share, out_weight, cots, freq_filter, mats[2:]
    )
    got = exchange(send)
    own, one, two, three, last, d_query = make_middle(
        where, got, x, freq_x, rate, own_skip, held, turned, back, freq_filter, *mats[2:], out_weight
    )
    last = exchange(last)
    mixed = make_mixed([own, shifted(one, 1), shifted(two, 2), shifted(three, 3)])
    d_key, d_value, filter_grad, skip_grad = make_finish(last, key_in, value_in)
    return (mixed, d_query, d_key, d_value, filter_grad, skip_grad.reshape(CHB))


def solution(mesh):
    in_specs = (
        P("ctx", "ch"),
        P("ctx", "ch"),
        P("ctx", "ch"),
        P(None, "ch"),
        P("ch"),
        P("ch"),
        P("ch", None),
        P("ctx", "ch"),
    )
    out_specs = (
        P("ctx", "ch"),
        P("ctx", "ch"),
        P("ctx", "ch"),
        P("ctx", "ch"),
        P("ctx", "ch"),
        P("ch"),
    )
    return jax.shard_map(local, mesh=mesh, in_specs=in_specs, out_specs=out_specs, check_vma=False)
```

```python
from functools import partial

import jax
import jax.numpy as jnp
import ml_dtypes
import numpy as np
from jax import lax
from jax.experimental import pallas as pl
from jax.experimental.pallas import tpu as pltpu
from jax.sharding import PartitionSpec as P

PANEL = 128
PANELS = 32
TURNS = 2 * PANELS
OWN = 32
PITCH = 40
CHB = 1024
SPLIT = 4
CHUNK = 256
GROUP = 8
TAIL = 16
F32 = jnp.float32
BF16 = jnp.bfloat16
LIMIT = 24 * 1024 * 1024


def tables():
    freq = np.arange(PANEL) + 0.5
    angle = 2 * np.pi * np.arange(PANEL)[:, None] * freq[None, :] / (2 * PANEL)
    turn = 2 * np.pi * np.arange(TURNS)[:, None] * np.arange(PANELS)[None, :] / TURNS
    cos, sin = np.cos(angle), np.sin(angle)
    inner = np.block([[cos, -sin], [sin, cos]])
    inner_back = np.concatenate([cos.T, -sin.T], axis=0) / (PANEL * TURNS)
    cos, sin = np.cos(turn), np.sin(turn)
    outer = np.concatenate([cos, -sin], axis=0)
    outer_back = np.block([[cos.T, -sin.T], [sin.T, cos.T]])
    return [m.astype(ml_dtypes.bfloat16) for m in (outer, inner, outer_back, inner_back)]


def dot(left, right):
    return jnp.dot(left, right, preferred_element_type=F32)


def dot_rows(left, right):
    return lax.dot_general(left, right, (((1,), (1,)), ((), ())), preferred_element_type=F32)


def spectrum(mid_ref, outer, inner, store):
    for c in range(0, OWN, 4):
        rows = []
        for b in (c, c + 2):
            pair = [mid_ref[0, pl.ds(b + q, PANELS, stride=PITCH), :].astype(BF16) for q in (0, 1)]
            both = dot(outer, jnp.concatenate(pair, axis=1)).astype(BF16)
            for q in (0, 1):
                one = both[:, q * PANEL : (q + 1) * PANEL]
                rows.append(jnp.concatenate([one[:TURNS], one[TURNS:]], axis=1))
        store(c, dot(jnp.concatenate(rows, axis=0), inner).astype(BF16))


def rows_of(freq_ref, c):
    both = freq_ref[pl.ds(c * TURNS, TURNS), :].astype(F32)
    return both[:, :PANEL], both[:, PANEL:]


def spread(c, columns, outer_back, mid_ref):
    back = dot(outer_back, jnp.concatenate(columns, axis=1))
    for part in (0, 1):
        for q in range(len(columns)):
            mid_ref[part, pl.ds(c + q, PANELS, stride=PITCH), :] = back[
                part * PANELS : (part + 1) * PANELS, q * PANEL : (q + 1) * PANEL
            ]


def gather_panels(mid_ref, inner_back, shift, store):
    lanes = lax.broadcasted_iota(jnp.int32, (1, PANEL), 1)
    sign = (1.0 - 2.0 * (lanes % 2).astype(F32)) * shift
    for a in range(0, PANELS, GROUP):
        parts = []
        for b in range(a, a + GROUP):
            real = mid_ref[0, pl.ds(b * PITCH, OWN), :]
            imag = mid_ref[1, pl.ds(b * PITCH, OWN), :]
            other = b - shift
            if 0 <= other < PANELS:
                there_real = mid_ref[0, pl.ds(other * PITCH, OWN), :]
                there_imag = mid_ref[1, pl.ds(other * PITCH, OWN), :]
                real = real - sign * there_imag
                imag = imag + sign * there_real
            parts.append(jnp.concatenate([real.astype(BF16), imag.astype(BF16)], axis=1))
        done = dot(jnp.concatenate(parts, axis=0), inner_back)
        for b in range(GROUP):
            store(a + b, done[b * OWN : (b + 1) * OWN])


def start_all(moves, sems, first=0):
    copies = [pltpu.make_async_copy(here, to, sems.at[first + n]) for n, (here, to) in enumerate(moves)]
    for copy in copies:
        copy.start()
    return copies


def wait_all(copies):
    for copy in copies:
        copy.wait()


def product_kernel(key_from, value_from, out_ref, key_ref, value_ref, sems):
    wait_all(start_all([(key_from, key_ref), (value_from, value_ref)], sems))
    product = key_ref[...].astype(F32) * value_ref[...].astype(F32)
    out_ref[...] = product.T.astype(BF16).reshape(PANELS, OWN, PANEL)


def filter_kernel(
    where_ref,
    raw_from,
    decay_from,
    skip_from,
    outer_from,
    inner_from,
    query_from,
    cot_from,
    weight_from,
    freq_to,
    rate_ref,
    own_skip_ref,
    outer_ref,
    inner_ref,
    turned_ref,
    share_to,
    freq_ref,
    raw_ref,
    decay_ref,
    skip_ref,
    query_ref,
    cot_ref,
    keep_ref,
    share_ref,
    mid_ref,
    sems,
):
    column = pl.ds(pl.multiple_of(lax.div(where_ref[0], SPLIT) * PANEL, PANEL), PANEL)
    moves = [(decay_from, decay_ref)]
    for n in range(SPLIT):
        rows = pl.ds(n * CHB, CHB)
        moves.append((raw_from.at[rows, column], raw_ref.at[rows, :]))
    moves += [(outer_from, outer_ref), (inner_from, inner_ref), (skip_from, skip_ref)]
    own = pl.ds(pl.multiple_of(where_ref[1] * CHB, CHB), CHB)
    moves += [(query_from, query_ref), (cot_from, cot_ref), (weight_from.at[:, own], keep_ref)]
    loads = start_all(moves, sems)
    place = lax.rem(where_ref[0], SPLIT) * OWN
    row = lax.broadcasted_iota(jnp.int32, (OWN, PANEL), 0)
    lane = lax.broadcasted_iota(jnp.int32, (OWN, PANEL), 1)
    mine = lane == row + place
    choose = mine.astype(BF16)
    loads[0].wait()

    def own_column(ref):
        line = ref[pl.ds(lax.div(where_ref[0], SPLIT), 1), :]
        column = jnp.sum(jnp.where(mine, line, 0.0), axis=1, keepdims=True)
        return jnp.broadcast_to(column, (OWN, PANEL))

    rate = own_column(decay_ref)
    rate_ref[...] = rate
    for n in range(SPLIT):
        loads[1 + n].wait()
        for a in range(n * GROUP, (n + 1) * GROUP, 4):
            chosen = dot_rows(choose, raw_ref[pl.ds(a * PANEL, 4 * PANEL), :])
            for b in range(4):
                spot = (lane + (a + b) * PANEL).astype(F32)
                taps = chosen[:, b * PANEL : (b + 1) * PANEL] * jnp.exp(-rate * spot)
                mid_ref[0, pl.ds((a + b) * PITCH, OWN), :] = taps
    wait_all(loads[1 + SPLIT : -2])
    own_skip_ref[...] = own_column(skip_ref)
    for c in range(0, CHB, CHUNK):
        at = pl.ds(c, CHUNK)
        turned_ref[at, :] = query_ref[:, at].astype(F32).T.astype(BF16)
    wait_all(loads[-2:])
    for c in range(0, CHB, CHUNK):
        at = pl.ds(c, CHUNK)
        share_ref[at, :] = dot_rows(keep_ref[at, :], cot_ref[...])
    writes = start_all([(share_ref, share_to)], sems, len(moves))

    def store(c, rows):
        part = pl.ds(c * TURNS, 4 * TURNS)
        freq_ref[part, :] = rows
        writes.extend(start_all([(freq_ref.at[part], freq_to.at[part])], sems, len(moves) + len(writes)))

    spectrum(mid_ref, outer_ref[...], inner_ref[...], store)
    wait_all(writes)


def forward_kernel(
    where_ref,
    x_ref,
    own_skip_ref,
    outer_ref,
    inner_ref,
    query_ref,
    cot1_ref,
    cot2_ref,
    cot3_ref,
    share_from,
    filter_from,
    outer_back_from,
    inner_back_from,
    weight_from,
    send_ref,
    freq_ref,
    back_ref,
    mid_ref,
    outer_back_ref,
    inner_back_ref,
    filter_ref,
    cot_ref,
    share_ref,
    weight_ref,
    sems,
):
    moves = [
        (outer_back_from, outer_back_ref),
        (inner_back_from, inner_back_ref),
        (filter_from, filter_ref),
    ]
    moves += [(ref, cot_ref.at[s]) for s, ref in enumerate((cot1_ref, cot2_ref, cot3_ref))]
    moves.append((share_from, share_ref))
    loads = start_all(moves, sems)

    def weight_copies(n):
        rows = pl.ds(pl.multiple_of(n * CHUNK, CHUNK), CHUNK)
        copies = []
        for s in range(1, SPLIT):
            block = lax.rem(where_ref[1] + SPLIT - s, SPLIT) * CHB
            columns = pl.ds(pl.multiple_of(block, CHB), CHB)
            sem = sems.at[len(moves) + (SPLIT - 1) * n + s - 1]
            copies.append(
                pltpu.make_async_copy(weight_from.at[rows, columns], weight_ref.at[s - 1, rows, :], sem)
            )
        return copies

    for n in range(CHB // CHUNK):
        for copy in weight_copies(n):
            copy.start()
    for a in range(PANELS):
        mid_ref[0, pl.ds(a * PITCH, OWN), :] = x_ref[a].astype(F32)

    def store(c, rows):
        freq_ref[pl.ds(c * TURNS, 4 * TURNS), :] = rows

    spectrum(mid_ref, outer_ref[...], inner_ref[...], store)
    wait_all(loads[:3])
    outer_back = outer_back_ref[...]
    for c in range(0, OWN, 2):
        columns = []
        for b in (c, c + 1):
            xr, xi = rows_of(freq_ref, b)
            hr, hi = rows_of(filter_ref, b)
            columns.append(
                jnp.concatenate(
                    [(hr * xr - hi * xi).astype(BF16), (hr * xi + hi * xr).astype(BF16)], axis=0
                )
            )
        spread(c, columns, outer_back, mid_ref)

    own_skip = own_skip_ref[...]

    def store_panel(a, value):
        send_ref[a, :OWN, :] = (value + own_skip * x_ref[a].astype(F32)).astype(BF16)

    gather_panels(mid_ref, inner_back_ref[...], 1, store_panel)
    wait_all(loads[3:])

    @pl.loop(0, CHB // CHUNK)
    def _(n):
        wait_all(weight_copies(n))
        at = pl.ds(pl.multiple_of(n * CHUNK, CHUNK), CHUNK)
        total = share_ref[at, :]
        for s in range(SPLIT - 1):
            total += dot_rows(weight_ref[s, at, :], cot_ref[s])
        back_ref[at, :] = total
        grad = (query_ref[at, :].astype(F32) * total).astype(BF16)
        for b in range(CHUNK // OWN):
            send_ref[n * (CHUNK // OWN) + b, OWN:, :] = grad[b * OWN : (b + 1) * OWN]


def middle_kernel(
    where_ref,
    got_ref,
    x_ref,
    freq_ref,
    rate_ref,
    own_skip_ref,
    outer_ref,
    inner_ref,
    query_ref,
    back_ref,
    filter_from,
    outer_back_from,
    inner_back_from,
    weight_from,
    own_to,
    one_to,
    two_to,
    three_to,
    send_to,
    d_query_to,
    outer_back_ref,
    inner_back_ref,
    filter_ref,
    spec_ref,
    mid_ref,
    lag_ref,
    gated_ref,
    d_query_ref,
    part_ref,
    send_ref,
    weight_ref,
    sems,
):
    moves = [
        (outer_back_from, outer_back_ref),
        (inner_back_from, inner_back_ref),
        (filter_from, filter_ref),
    ]
    loads = start_all(moves, sems)
    writes = []

    def write(this, to):
        writes.extend(start_all([(this, to)], sems, len(moves) + SPLIT + len(writes)))

    def weight_copy(n, s):
        block = lax.rem(where_ref[1] + s, SPLIT) * CHB
        columns = pl.ds(pl.multiple_of(block, CHB), CHB)
        return pltpu.make_async_copy(
            weight_from.at[:, columns], weight_ref.at[n], sems.at[len(moves) + n]
        )

    for n, s in enumerate((2, 1, 3, 0)):
        weight_copy(n, s).start()
    for c in range(0, CHB, CHUNK):
        at = pl.ds(c, CHUNK)
        block = got_ref[pl.ds(c // OWN, CHUNK // OWN), :OWN, :].reshape(CHUNK, PANEL)
        convolved = block.astype(F32)
        gated_ref[:, at] = (query_ref[at, :].astype(F32) * convolved).T.astype(BF16)
        d_query_ref[:, at] = (back_ref[at, :] * convolved).T.astype(BF16)
    write(d_query_ref, d_query_to)
    for a in range(PANELS):
        mid_ref[0, pl.ds(a * PITCH, OWN), :] = got_ref[a, OWN:, :].astype(F32)

    def store(c, rows):
        spec_ref[pl.ds(c * TURNS, 4 * TURNS), :] = rows

    spectrum(mid_ref, outer_ref[...], inner_ref[...], store)
    wait_all(loads)
    outer_back = outer_back_ref[...]
    for c in range(0, OWN, 2):
        columns = {0: [], 1: []}
        for b in (c, c + 1):
            gr, gi = rows_of(spec_ref, b)
            for n, other_ref in enumerate((filter_ref, freq_ref)):
                hr, hi = rows_of(other_ref, b)
                columns[n].append(
                    jnp.concatenate(
                        [(gr * hr + gi * hi).astype(BF16), (gi * hr - gr * hi).astype(BF16)], axis=0
                    )
                )
        spread(c, columns[0], outer_back, mid_ref)
        spread(c, columns[1], outer_back, lag_ref)
    own_skip = own_skip_ref[...]
    sums = [jnp.zeros((OWN, PANEL), F32)]

    def store_input(a, value):
        grad = got_ref[a, OWN:, :].astype(F32)
        sums[0] += grad * x_ref[a].astype(F32)
        send_ref[a, :OWN, :] = (value + own_skip * grad).astype(BF16)

    gather_panels(mid_ref, inner_back_ref[...], -1, store_input)
    rate = rate_ref[...]
    lane = lax.broadcasted_iota(jnp.int32, (OWN, PANEL), 1)
    row = lax.broadcasted_iota(jnp.int32, (OWN, PANEL), 0)
    total = jnp.sum(sums[0], axis=1, keepdims=True)
    place = lax.rem(where_ref[0], SPLIT) * OWN
    line = jnp.sum(jnp.where(lane == row + place, total, 0.0), axis=0, keepdims=True)
    high = line.astype(BF16).astype(F32)
    index = lax.broadcasted_iota(jnp.int32, (TAIL, PANEL), 0)
    tail = jnp.where(index == 0, high, jnp.where(index == 1, line - high, 0.0)).astype(BF16)

    def store_lag(a, value):
        window = jnp.exp(-rate * (lane + a * PANEL).astype(F32))
        send_ref[a, OWN : 2 * OWN, :] = (value * window).astype(BF16)
        send_ref[a, 2 * OWN :, :] = tail
        if (a + 1) % GROUP == 0:
            part = pl.ds(a + 1 - GROUP, GROUP)
            write(send_ref.at[part], send_to.at[part])

    gather_panels(lag_ref, inner_back_ref[...], -1, store_lag)
    outs = (two_to, one_to, three_to, own_to)
    base = len(moves) + SPLIT + len(writes)
    writes += [
        pltpu.make_async_copy(part_ref.at[n], to, sems.at[base + n]) for n, to in enumerate(outs)
    ]

    @pl.loop(0, SPLIT)
    def _(n):
        weight_copy(n, 0).wait()
        for c in range(0, CHB, CHUNK):
            at = pl.ds(c, CHUNK)
            part_ref[n, :, at] = dot(gated_ref[...], weight_ref[n, :, at]).astype(BF16)
        for k in range(SPLIT):

            @pl.when(n == k)
            def _():
                writes[k - SPLIT].start()

    wait_all(writes)


def pair_kernel(own_from, two_ref, pair_ref, own_ref, sem):
    load = pltpu.make_async_copy(own_from, own_ref, sem)
    load.start()
    load.wait()
    for c in range(0, CHB, CHUNK):
        at = pl.ds(c, CHUNK)
        pair_ref[:, at] = own_ref[:, at].astype(F32) + two_ref[:, at].astype(F32)


def finish_kernel(
    got_ref,
    key_ref,
    value_ref,
    pair_ref,
    one_ref,
    three_ref,
    mixed_ref,
    d_key_ref,
    d_value_ref,
    lag_ref,
    skip_grad_ref,
):
    for c in range(0, CHB, CHUNK):
        at = pl.ds(c, CHUNK)
        block = pl.ds(c // OWN, CHUNK // OWN)
        lag_ref[:, at] = got_ref[block, OWN : 2 * OWN, :].reshape(CHUNK, PANEL).astype(F32).T
        grad = got_ref[block, :OWN, :].reshape(CHUNK, PANEL).astype(F32).T
        d_key_ref[:, at] = (grad * value_ref[:, at].astype(F32)).astype(BF16)
        d_value_ref[:, at] = (grad * key_ref[:, at].astype(F32)).astype(BF16)
        both = one_ref[:, at].astype(F32) + three_ref[:, at].astype(F32)
        mixed_ref[:, at] = (pair_ref[:, at] + both).astype(BF16)
    for r in range(PANELS // SPLIT):
        line = jnp.zeros((1, PANEL), F32)
        for b in range(SPLIT):
            tail = got_ref[r * SPLIT + b, 2 * OWN :, :].astype(F32)
            line += tail[0:1] + tail[1:2]
        skip_grad_ref[pl.ds(r, 1), :] = line


VMEM = pl.BlockSpec(memory_space=pltpu.VMEM)
SMEM = pl.BlockSpec(memory_space=pltpu.SMEM)
HBM = pl.BlockSpec(memory_space=pltpu.HBM)
ANY = pl.BlockSpec(memory_space=pl.ANY)
NEAR = pl.BlockSpec(memory_space=pltpu.VMEM)
FREQ = (OWN * TURNS, 2 * PANEL)
MID = pltpu.VMEM((2, PANELS * PITCH, PANEL), F32)
BLOCK = (PANEL, CHB)
SENT = (PANELS, 2 * OWN, PANEL)
LAST = (PANELS, 2 * OWN + TAIL, PANEL)


def shape(dims, kind):
    return jax.ShapeDtypeStruct(dims, kind)


def here(dims, kind):
    return pltpu.VMEM(dims, kind)


def far(dims, kind):
    return pltpu.HBM(dims, kind)


def call(kernel, in_specs, out_shape, scratch, flops, name, out_specs=None):
    run = pl.pallas_call(
        kernel,
        in_specs=in_specs,
        out_specs=out_specs or jax.tree.map(lambda _: VMEM, out_shape),
        out_shape=out_shape,
        scratch_shapes=scratch,
        compiler_params=pltpu.CompilerParams(vmem_limit_bytes=LIMIT),
        cost_estimate=pl.CostEstimate(flops=flops, bytes_accessed=1 << 20, transcendentals=0),
        name=name,
    )

    def placed(arg, spec):
        if spec is HBM:
            return pltpu.with_memory_space_constraint(arg, pltpu.HBM)
        if spec is NEAR:
            return pltpu.with_memory_space_constraint(arg, pltpu.VMEM)
        return arg

    def bound(*args):
        return run(*(placed(arg, spec) for arg, spec in zip(args, in_specs, strict=True)))

    return bound


def sems(count):
    return pltpu.SemaphoreType.DMA((count,))


def make_product(key_in, value_in):
    scratch = [pltpu.VMEM(BLOCK, BF16), pltpu.VMEM(BLOCK, BF16), sems(2)]
    out = shape((PANELS, OWN, PANEL), BF16)
    return call(product_kernel, [HBM] * 2, out, scratch, 1 << 20, "product")(key_in, value_in)


def make_filter(where, filter_raw, decay, skip, outer, inner, query, cot, weight):
    out = [far(FREQ, BF16), here((OWN, PANEL), F32), here((OWN, PANEL), F32)]
    out += [here(m.shape, BF16) for m in (outer, inner)] + [here((CHB, PANEL), BF16)]
    out.append(far((CHB, PANEL), F32))
    scratch = [
        pltpu.VMEM(FREQ, BF16),
        pltpu.VMEM((PANELS * PANEL, PANEL), BF16),
        pltpu.VMEM(decay.shape, F32),
        pltpu.VMEM(skip.shape, F32),
        pltpu.VMEM(BLOCK, BF16),
        pltpu.VMEM(BLOCK, BF16),
        pltpu.VMEM((CHB, CHB), BF16),
        pltpu.VMEM((CHB, PANEL), F32),
        MID,
        sems(8 + SPLIT + OWN // 4),
    ]
    specs = [SMEM] + [HBM] * 8
    return call(filter_kernel, specs, out, scratch, 1 << 32, "taps", [HBM] + [VMEM] * 5 + [HBM])(
        where, filter_raw, decay, skip, outer, inner, query, cot, weight
    )


def make_forward(where, x, own_skip, held, query, share, weight, cots, freq_filter, back_mats):
    out = [shape(SENT, BF16), here(FREQ, BF16), here((CHB, PANEL), F32)]
    scratch = [MID] + [pltpu.VMEM(m.shape, BF16) for m in back_mats]
    scratch += [pltpu.VMEM(FREQ, BF16), pltpu.VMEM((SPLIT - 1, *BLOCK), BF16)]
    scratch += [pltpu.VMEM((CHB, PANEL), F32), pltpu.VMEM((SPLIT - 1, CHB, CHB), BF16)]
    scratch.append(sems(4 + (SPLIT - 1) * (1 + CHB // CHUNK)))
    specs = [SMEM] + [VMEM] * 5 + [ANY] * 3 + [HBM] * 5
    return call(forward_kernel, specs, out, scratch, 1 << 33, "forward")(
        where, x, own_skip, *held, query, *cots, share, freq_filter, *back_mats, weight
    )


def make_middle(where, got, x, freq_x, rate, own_skip, held, query, back, *rest):
    out = [far(BLOCK, BF16)] * 4 + [far(LAST, BF16), far(BLOCK, BF16)]
    scratch = [pltpu.VMEM(m.shape, BF16) for m in rest[1:3]]
    scratch += [pltpu.VMEM(FREQ, BF16), pltpu.VMEM(FREQ, BF16), MID, MID]
    scratch += [pltpu.VMEM(BLOCK, BF16)] * 2
    scratch += [pltpu.VMEM((SPLIT, *BLOCK), BF16), pltpu.VMEM(LAST, BF16)]
    scratch += [pltpu.VMEM((SPLIT, CHB, CHB), BF16), sems(4 + 2 * SPLIT + PANELS // GROUP)]
    specs = [SMEM] + [VMEM] * 9 + [HBM] * 4
    return call(middle_kernel, specs, out, scratch, 1 << 33, "middle", [HBM] * 6)(
        where, got, x, freq_x, rate, own_skip, *held, query, back, *rest
    )


def make_pair(own, two):
    scratch = [pltpu.VMEM(BLOCK, BF16), pltpu.SemaphoreType.DMA]
    return call(pair_kernel, [HBM, VMEM], here(BLOCK, F32), scratch, 1 << 36, "pair")(own, two)


def make_finish(got, key_in, value_in, pair, one, three):
    out = [shape(BLOCK, BF16)] * 3 + [shape(BLOCK, F32), shape((CHB // PANEL, PANEL), F32)]
    return call(finish_kernel, [VMEM] * 6, out, [], 1 << 20, "finish")(
        got, key_in, value_in, pair, one, three
    )


def shifted(value, step):
    return lax.ppermute(value, "ch", [(i, (i + step) % SPLIT) for i in range(SPLIT)])


def exchange(value):
    return lax.all_to_all(value, "ctx", 0, 0)


def local(query, key_in, value_in, filter_raw, decay, skip, out_weight, cotangent):
    mats = [jnp.asarray(m) for m in tables()]
    where = jnp.stack([lax.axis_index("ctx"), lax.axis_index("ch")]).astype(jnp.int32)
    lines = (CHB // PANEL, PANEL)
    cots = [shifted(cotangent, s) for s in (1, 2, 3)]
    x = exchange(make_product(key_in, value_in))
    lined = (decay.reshape(lines), skip.reshape(lines))
    freq_filter, rate, own_skip, *held, turned, share = make_filter(
        where, filter_raw, *lined, *mats[:2], query, cotangent, out_weight
    )
    send, freq_x, back = make_forward(
        where, x, own_skip, held, turned, share, out_weight, cots, freq_filter, mats[2:]
    )
    got = exchange(send)
    own, one, two, three, last, d_query = make_middle(
        where, got, x, freq_x, rate, own_skip, held, turned, back, freq_filter, *mats[2:], out_weight
    )
    last = exchange(last)
    pair = make_pair(own, shifted(two, 2))
    mixed, d_key, d_value, filter_grad, skip_grad = make_finish(
        last, key_in, value_in, pair, shifted(one, 1), shifted(three, 3)
    )
    return (mixed, d_query, d_key, d_value, filter_grad, skip_grad.reshape(CHB))


def solution(mesh):
    in_specs = (
        P("ctx", "ch"),
        P("ctx", "ch"),
        P("ctx", "ch"),
        P(None, "ch"),
        P("ch"),
        P("ch"),
        P("ch", None),
        P("ctx", "ch"),
    )
    out_specs = (
        P("ctx", "ch"),
        P("ctx", "ch"),
        P("ctx", "ch"),
        P("ctx", "ch"),
        P("ctx", "ch"),
        P("ch"),
    )
    return jax.shard_map(local, mesh=mesh, in_specs=in_specs, out_specs=out_specs, check_vma=False)
```

```python
from functools import partial

import jax
import jax.numpy as jnp
import ml_dtypes
import numpy as np
from jax import lax
from jax.experimental import pallas as pl
from jax.experimental.pallas import tpu as pltpu
from jax.sharding import PartitionSpec as P

PANEL = 128
PANELS = 32
TURNS = 2 * PANELS
OWN = 32
PITCH = 40
CHB = 1024
SPLIT = 4
CHUNK = 256
GROUP = 8
TAIL = 16
F32 = jnp.float32
BF16 = jnp.bfloat16
LIMIT = 24 * 1024 * 1024


def tables():
    freq = np.arange(PANEL) + 0.5
    angle = 2 * np.pi * np.arange(PANEL)[:, None] * freq[None, :] / (2 * PANEL)
    turn = 2 * np.pi * np.arange(TURNS)[:, None] * np.arange(PANELS)[None, :] / TURNS
    cos, sin = np.cos(angle), np.sin(angle)
    inner = np.block([[cos, -sin], [sin, cos]])
    inner_back = np.concatenate([cos.T, -sin.T], axis=0) / (PANEL * TURNS)
    cos, sin = np.cos(turn), np.sin(turn)
    outer = np.concatenate([cos, -sin], axis=0)
    outer_back = np.block([[cos.T, -sin.T], [sin.T, cos.T]])
    return [m.astype(ml_dtypes.bfloat16) for m in (outer, inner, outer_back, inner_back)]


def dot(left, right):
    return jnp.dot(left, right, preferred_element_type=F32)


def dot_rows(left, right):
    return lax.dot_general(left, right, (((1,), (1,)), ((), ())), preferred_element_type=F32)


def spectrum(mid_ref, outer, inner, store):
    for c in range(0, OWN, 4):
        rows = []
        for b in (c, c + 2):
            pair = [mid_ref[0, pl.ds(b + q, PANELS, stride=PITCH), :].astype(BF16) for q in (0, 1)]
            both = dot(outer, jnp.concatenate(pair, axis=1)).astype(BF16)
            for q in (0, 1):
                one = both[:, q * PANEL : (q + 1) * PANEL]
                rows.append(jnp.concatenate([one[:TURNS], one[TURNS:]], axis=1))
        store(c, dot(jnp.concatenate(rows, axis=0), inner).astype(BF16))


def rows_of(freq_ref, c):
    both = freq_ref[pl.ds(c * TURNS, TURNS), :].astype(F32)
    return both[:, :PANEL], both[:, PANEL:]


def spread(c, columns, outer_back, mid_ref):
    back = dot(outer_back, jnp.concatenate(columns, axis=1))
    for part in (0, 1):
        for q in range(len(columns)):
            mid_ref[part, pl.ds(c + q, PANELS, stride=PITCH), :] = back[
                part * PANELS : (part + 1) * PANELS, q * PANEL : (q + 1) * PANEL
            ]


def gather_panels(mid_ref, inner_back, shift, store):
    lanes = lax.broadcasted_iota(jnp.int32, (1, PANEL), 1)
    sign = (1.0 - 2.0 * (lanes % 2).astype(F32)) * shift
    for a in range(0, PANELS, GROUP):
        parts = []
        for b in range(a, a + GROUP):
            real = mid_ref[0, pl.ds(b * PITCH, OWN), :]
            imag = mid_ref[1, pl.ds(b * PITCH, OWN), :]
            other = b - shift
            if 0 <= other < PANELS:
                there_real = mid_ref[0, pl.ds(other * PITCH, OWN), :]
                there_imag = mid_ref[1, pl.ds(other * PITCH, OWN), :]
                real = real - sign * there_imag
                imag = imag + sign * there_real
            parts.append(jnp.concatenate([real.astype(BF16), imag.astype(BF16)], axis=1))
        done = dot(jnp.concatenate(parts, axis=0), inner_back)
        for b in range(GROUP):
            store(a + b, done[b * OWN : (b + 1) * OWN])


def start_all(moves, sems, first=0):
    copies = [pltpu.make_async_copy(here, to, sems.at[first + n]) for n, (here, to) in enumerate(moves)]
    for copy in copies:
        copy.start()
    return copies


def wait_all(copies):
    for copy in copies:
        copy.wait()


def product_kernel(key_from, value_from, out_ref, key_ref, value_ref, sems):
    wait_all(start_all([(key_from, key_ref), (value_from, value_ref)], sems))
    product = key_ref[...].astype(F32) * value_ref[...].astype(F32)
    out_ref[...] = product.T.astype(BF16).reshape(PANELS, OWN, PANEL)


def filter_kernel(
    where_ref,
    raw_from,
    decay_from,
    skip_from,
    outer_from,
    inner_from,
    query_from,
    cot_from,
    weight_from,
    freq_to,
    rate_ref,
    own_skip_ref,
    outer_ref,
    inner_ref,
    turned_ref,
    share_to,
    freq_ref,
    raw_ref,
    decay_ref,
    skip_ref,
    query_ref,
    cot_ref,
    keep_ref,
    share_ref,
    mid_ref,
    sems,
):
    column = pl.ds(pl.multiple_of(lax.div(where_ref[0], SPLIT) * PANEL, PANEL), PANEL)
    moves = [(decay_from, decay_ref)]
    for n in range(SPLIT):
        rows = pl.ds(n * CHB, CHB)
        moves.append((raw_from.at[rows, column], raw_ref.at[rows, :]))
    moves += [(outer_from, outer_ref), (inner_from, inner_ref), (skip_from, skip_ref)]
    own = pl.ds(pl.multiple_of(where_ref[1] * CHB, CHB), CHB)
    moves += [(query_from, query_ref), (cot_from, cot_ref), (weight_from.at[:, own], keep_ref)]
    loads = start_all(moves, sems)
    place = lax.rem(where_ref[0], SPLIT) * OWN
    row = lax.broadcasted_iota(jnp.int32, (OWN, PANEL), 0)
    lane = lax.broadcasted_iota(jnp.int32, (OWN, PANEL), 1)
    mine = lane == row + place
    choose = mine.astype(BF16)
    loads[0].wait()

    def own_column(ref):
        line = ref[pl.ds(lax.div(where_ref[0], SPLIT), 1), :]
        column = jnp.sum(jnp.where(mine, line, 0.0), axis=1, keepdims=True)
        return jnp.broadcast_to(column, (OWN, PANEL))

    rate = own_column(decay_ref)
    rate_ref[...] = rate
    for n in range(SPLIT):
        loads[1 + n].wait()
        for a in range(n * GROUP, (n + 1) * GROUP, 4):
            chosen = dot_rows(choose, raw_ref[pl.ds(a * PANEL, 4 * PANEL), :])
            for b in range(4):
                spot = (lane + (a + b) * PANEL).astype(F32)
                taps = chosen[:, b * PANEL : (b + 1) * PANEL] * jnp.exp(-rate * spot)
                mid_ref[0, pl.ds((a + b) * PITCH, OWN), :] = taps
    wait_all(loads[1 + SPLIT : -2])
    own_skip_ref[...] = own_column(skip_ref)
    for c in range(0, CHB, CHUNK):
        at = pl.ds(c, CHUNK)
        turned_ref[at, :] = query_ref[:, at].astype(F32).T.astype(BF16)
    wait_all(loads[-2:])
    for c in range(0, CHB, CHUNK):
        at = pl.ds(c, CHUNK)
        share_ref[at, :] = dot_rows(keep_ref[at, :], cot_ref[...])
    writes = start_all([(share_ref, share_to)], sems, len(moves))

    def store(c, rows):
        part = pl.ds(c * TURNS, 4 * TURNS)
        freq_ref[part, :] = rows
        writes.extend(start_all([(freq_ref.at[part], freq_to.at[part])], sems, len(moves) + len(writes)))

    spectrum(mid_ref, outer_ref[...], inner_ref[...], store)
    wait_all(writes)


def forward_kernel(
    where_ref,
    x_ref,
    own_skip_ref,
    outer_ref,
    inner_ref,
    query_ref,
    cot1_ref,
    cot2_ref,
    cot3_ref,
    share_from,
    filter_from,
    outer_back_from,
    inner_back_from,
    weight_from,
    send_ref,
    freq_ref,
    back_ref,
    mid_ref,
    outer_back_ref,
    inner_back_ref,
    filter_ref,
    cot_ref,
    share_ref,
    weight_ref,
    sems,
):
    moves = [
        (outer_back_from, outer_back_ref),
        (inner_back_from, inner_back_ref),
        (filter_from, filter_ref),
    ]
    moves += [(ref, cot_ref.at[s]) for s, ref in enumerate((cot1_ref, cot2_ref, cot3_ref))]
    moves.append((share_from, share_ref))
    loads = start_all(moves, sems)

    def weight_copies(n):
        rows = pl.ds(pl.multiple_of(n * CHUNK, CHUNK), CHUNK)
        copies = []
        for s in range(1, SPLIT):
            block = lax.rem(where_ref[1] + SPLIT - s, SPLIT) * CHB
            columns = pl.ds(pl.multiple_of(block, CHB), CHB)
            sem = sems.at[len(moves) + (SPLIT - 1) * n + s - 1]
            copies.append(
                pltpu.make_async_copy(weight_from.at[rows, columns], weight_ref.at[s - 1, rows, :], sem)
            )
        return copies

    for n in range(CHB // CHUNK):
        for copy in weight_copies(n):
            copy.start()
    for a in range(PANELS):
        mid_ref[0, pl.ds(a * PITCH, OWN), :] = x_ref[a].astype(F32)

    def store(c, rows):
        freq_ref[pl.ds(c * TURNS, 4 * TURNS), :] = rows

    spectrum(mid_ref, outer_ref[...], inner_ref[...], store)
    wait_all(loads[:3])
    outer_back = outer_back_ref[...]
    for c in range(0, OWN, 2):
        columns = []
        for b in (c, c + 1):
            xr, xi = rows_of(freq_ref, b)
            hr, hi = rows_of(filter_ref, b)
            columns.append(
                jnp.concatenate(
                    [(hr * xr - hi * xi).astype(BF16), (hr * xi + hi * xr).astype(BF16)], axis=0
                )
            )
        spread(c, columns, outer_back, mid_ref)

    own_skip = own_skip_ref[...]

    def store_panel(a, value):
        send_ref[a, :OWN, :] = (value + own_skip * x_ref[a].astype(F32)).astype(BF16)

    gather_panels(mid_ref, inner_back_ref[...], 1, store_panel)
    wait_all(loads[3:])

    @pl.loop(0, CHB // CHUNK)
    def _(n):
        wait_all(weight_copies(n))
        at = pl.ds(pl.multiple_of(n * CHUNK, CHUNK), CHUNK)
        total = share_ref[at, :]
        for s in range(SPLIT - 1):
            total += dot_rows(weight_ref[s, at, :], cot_ref[s])
        back_ref[at, :] = total
        grad = (query_ref[at, :].astype(F32) * total).astype(BF16)
        for b in range(CHUNK // OWN):
            send_ref[n * (CHUNK // OWN) + b, OWN:, :] = grad[b * OWN : (b + 1) * OWN]


def middle_kernel(
    where_ref,
    got_ref,
    x_ref,
    freq_ref,
    rate_ref,
    own_skip_ref,
    outer_ref,
    inner_ref,
    query_ref,
    back_ref,
    filter_from,
    outer_back_from,
    inner_back_from,
    weight_from,
    own_to,
    one_to,
    two_to,
    three_to,
    send_to,
    d_query_to,
    outer_back_ref,
    inner_back_ref,
    filter_ref,
    spec_ref,
    mid_ref,
    lag_ref,
    gated_ref,
    d_query_ref,
    part_ref,
    send_ref,
    weight_ref,
    sems,
):
    moves = [
        (outer_back_from, outer_back_ref),
        (inner_back_from, inner_back_ref),
        (filter_from, filter_ref),
    ]
    loads = start_all(moves, sems)
    writes = []

    def write(this, to):
        writes.extend(start_all([(this, to)], sems, len(moves) + SPLIT + len(writes)))

    def weight_copy(n, s):
        block = lax.rem(where_ref[1] + s, SPLIT) * CHB
        columns = pl.ds(pl.multiple_of(block, CHB), CHB)
        return pltpu.make_async_copy(
            weight_from.at[:, columns], weight_ref.at[n], sems.at[len(moves) + n]
        )

    for n, s in enumerate((2, 1, 3, 0)):
        weight_copy(n, s).start()
    for c in range(0, CHB, CHUNK):
        at = pl.ds(c, CHUNK)
        block = got_ref[pl.ds(c // OWN, CHUNK // OWN), :OWN, :].reshape(CHUNK, PANEL)
        convolved = block.astype(F32)
        gated_ref[:, at] = (query_ref[at, :].astype(F32) * convolved).T.astype(BF16)
        d_query_ref[:, at] = (back_ref[at, :] * convolved).T.astype(BF16)
    write(d_query_ref, d_query_to)
    for a in range(PANELS):
        mid_ref[0, pl.ds(a * PITCH, OWN), :] = got_ref[a, OWN:, :].astype(F32)

    def store(c, rows):
        spec_ref[pl.ds(c * TURNS, 4 * TURNS), :] = rows

    spectrum(mid_ref, outer_ref[...], inner_ref[...], store)
    wait_all(loads)
    outer_back = outer_back_ref[...]
    for c in range(0, OWN, 2):
        columns = {0: [], 1: []}
        for b in (c, c + 1):
            gr, gi = rows_of(spec_ref, b)
            for n, other_ref in enumerate((filter_ref, freq_ref)):
                hr, hi = rows_of(other_ref, b)
                columns[n].append(
                    jnp.concatenate(
                        [(gr * hr + gi * hi).astype(BF16), (gi * hr - gr * hi).astype(BF16)], axis=0
                    )
                )
        spread(c, columns[0], outer_back, mid_ref)
        spread(c, columns[1], outer_back, lag_ref)
    own_skip = own_skip_ref[...]
    sums = [jnp.zeros((OWN, PANEL), F32)]

    def store_input(a, value):
        grad = got_ref[a, OWN:, :].astype(F32)
        sums[0] += grad * x_ref[a].astype(F32)
        send_ref[a, :OWN, :] = (value + own_skip * grad).astype(BF16)

    gather_panels(mid_ref, inner_back_ref[...], -1, store_input)
    rate = rate_ref[...]
    lane = lax.broadcasted_iota(jnp.int32, (OWN, PANEL), 1)
    row = lax.broadcasted_iota(jnp.int32, (OWN, PANEL), 0)
    total = jnp.sum(sums[0], axis=1, keepdims=True)
    place = lax.rem(where_ref[0], SPLIT) * OWN
    line = jnp.sum(jnp.where(lane == row + place, total, 0.0), axis=0, keepdims=True)
    high = line.astype(BF16).astype(F32)
    index = lax.broadcasted_iota(jnp.int32, (TAIL, PANEL), 0)
    tail = jnp.where(index == 0, high, jnp.where(index == 1, line - high, 0.0)).astype(BF16)

    def store_lag(a, value):
        window = jnp.exp(-rate * (lane + a * PANEL).astype(F32))
        send_ref[a, OWN : 2 * OWN, :] = (value * window).astype(BF16)
        send_ref[a, 2 * OWN :, :] = tail
        if (a + 1) % GROUP == 0:
            part = pl.ds(a + 1 - GROUP, GROUP)
            write(send_ref.at[part], send_to.at[part])

    gather_panels(lag_ref, inner_back_ref[...], -1, store_lag)
    outs = (two_to, one_to, three_to, own_to)
    base = len(moves) + SPLIT + len(writes)
    writes += [
        pltpu.make_async_copy(part_ref.at[n], to, sems.at[base + n]) for n, to in enumerate(outs)
    ]

    @pl.loop(0, SPLIT)
    def _(n):
        weight_copy(n, 0).wait()
        for c in range(0, CHB, CHUNK):
            at = pl.ds(c, CHUNK)
            part_ref[n, :, at] = dot(gated_ref[...], weight_ref[n, :, at]).astype(BF16)
        for k in range(SPLIT):

            @pl.when(n == k)
            def _():
                writes[k - SPLIT].start()

    wait_all(writes)


def pair_kernel(own_from, two_ref, pair_ref, own_ref, sem):
    load = pltpu.make_async_copy(own_from, own_ref, sem)
    load.start()
    load.wait()
    for c in range(0, CHB, CHUNK):
        at = pl.ds(c, CHUNK)
        pair_ref[:, at] = own_ref[:, at].astype(F32) + two_ref[:, at].astype(F32)


def finish_kernel(
    got_ref,
    key_ref,
    value_ref,
    pair_ref,
    one_ref,
    three_ref,
    mixed_to,
    d_key_to,
    d_value_to,
    lag_to,
    skip_grad_ref,
    mixed_ref,
    d_key_ref,
    d_value_ref,
    lag_ref,
    sems,
):
    writes = []
    for c in range(0, CHB, CHUNK):
        at = pl.ds(c, CHUNK)
        block = pl.ds(c // OWN, CHUNK // OWN)
        lag_ref[:, at] = got_ref[block, OWN : 2 * OWN, :].reshape(CHUNK, PANEL).astype(F32).T
        grad = got_ref[block, :OWN, :].reshape(CHUNK, PANEL).astype(F32).T
        d_key_ref[:, at] = (grad * value_ref[:, at].astype(F32)).astype(BF16)
        d_value_ref[:, at] = (grad * key_ref[:, at].astype(F32)).astype(BF16)
        both = one_ref[:, at].astype(F32) + three_ref[:, at].astype(F32)
        mixed_ref[:, at] = (pair_ref[:, at] + both).astype(BF16)
        outs = ((lag_ref, lag_to), (d_key_ref, d_key_to), (d_value_ref, d_value_to), (mixed_ref, mixed_to))
        moves = [(this.at[:, at], to.at[:, at]) for this, to in outs]
        writes += start_all(moves, sems, len(writes))
    for r in range(PANELS // SPLIT):
        line = jnp.zeros((1, PANEL), F32)
        for b in range(SPLIT):
            tail = got_ref[r * SPLIT + b, 2 * OWN :, :].astype(F32)
            line += tail[0:1] + tail[1:2]
        skip_grad_ref[pl.ds(r, 1), :] = line
    wait_all(writes)


VMEM = pl.BlockSpec(memory_space=pltpu.VMEM)
SMEM = pl.BlockSpec(memory_space=pltpu.SMEM)
HBM = pl.BlockSpec(memory_space=pltpu.HBM)
ANY = pl.BlockSpec(memory_space=pl.ANY)
NEAR = pl.BlockSpec(memory_space=pltpu.VMEM)
FREQ = (OWN * TURNS, 2 * PANEL)
MID = pltpu.VMEM((2, PANELS * PITCH, PANEL), F32)
BLOCK = (PANEL, CHB)
SENT = (PANELS, 2 * OWN, PANEL)
LAST = (PANELS, 2 * OWN + TAIL, PANEL)


def shape(dims, kind):
    return jax.ShapeDtypeStruct(dims, kind)


def here(dims, kind):
    return pltpu.VMEM(dims, kind)


def far(dims, kind):
    return pltpu.HBM(dims, kind)


def call(kernel, in_specs, out_shape, scratch, flops, name, out_specs=None):
    run = pl.pallas_call(
        kernel,
        in_specs=in_specs,
        out_specs=out_specs or jax.tree.map(lambda _: VMEM, out_shape),
        out_shape=out_shape,
        scratch_shapes=scratch,
        compiler_params=pltpu.CompilerParams(vmem_limit_bytes=LIMIT),
        cost_estimate=pl.CostEstimate(flops=flops, bytes_accessed=1 << 20, transcendentals=0),
        name=name,
    )

    def placed(arg, spec):
        if spec is HBM:
            return pltpu.with_memory_space_constraint(arg, pltpu.HBM)
        if spec is NEAR:
            return pltpu.with_memory_space_constraint(arg, pltpu.VMEM)
        return arg

    def bound(*args):
        return run(*(placed(arg, spec) for arg, spec in zip(args, in_specs, strict=True)))

    return bound


def sems(count):
    return pltpu.SemaphoreType.DMA((count,))


def make_product(key_in, value_in):
    scratch = [pltpu.VMEM(BLOCK, BF16), pltpu.VMEM(BLOCK, BF16), sems(2)]
    out = shape((PANELS, OWN, PANEL), BF16)
    return call(product_kernel, [HBM] * 2, out, scratch, 1 << 20, "product")(key_in, value_in)


def make_filter(where, filter_raw, decay, skip, outer, inner, query, cot, weight):
    out = [far(FREQ, BF16), here((OWN, PANEL), F32), here((OWN, PANEL), F32)]
    out += [here(m.shape, BF16) for m in (outer, inner)] + [here((CHB, PANEL), BF16)]
    out.append(far((CHB, PANEL), F32))
    scratch = [
        pltpu.VMEM(FREQ, BF16),
        pltpu.VMEM((PANELS * PANEL, PANEL), BF16),
        pltpu.VMEM(decay.shape, F32),
        pltpu.VMEM(skip.shape, F32),
        pltpu.VMEM(BLOCK, BF16),
        pltpu.VMEM(BLOCK, BF16),
        pltpu.VMEM((CHB, CHB), BF16),
        pltpu.VMEM((CHB, PANEL), F32),
        MID,
        sems(8 + SPLIT + OWN // 4),
    ]
    specs = [SMEM] + [HBM] * 8
    return call(filter_kernel, specs, out, scratch, 1 << 32, "taps", [HBM] + [VMEM] * 5 + [HBM])(
        where, filter_raw, decay, skip, outer, inner, query, cot, weight
    )


def make_forward(where, x, own_skip, held, query, share, weight, cots, freq_filter, back_mats):
    out = [shape(SENT, BF16), here(FREQ, BF16), here((CHB, PANEL), F32)]
    scratch = [MID] + [pltpu.VMEM(m.shape, BF16) for m in back_mats]
    scratch += [pltpu.VMEM(FREQ, BF16), pltpu.VMEM((SPLIT - 1, *BLOCK), BF16)]
    scratch += [pltpu.VMEM((CHB, PANEL), F32), pltpu.VMEM((SPLIT - 1, CHB, CHB), BF16)]
    scratch.append(sems(4 + (SPLIT - 1) * (1 + CHB // CHUNK)))
    specs = [SMEM] + [VMEM] * 5 + [ANY] * 3 + [HBM] * 5
    return call(forward_kernel, specs, out, scratch, 1 << 33, "forward")(
        where, x, own_skip, *held, query, *cots, share, freq_filter, *back_mats, weight
    )


def make_middle(where, got, x, freq_x, rate, own_skip, held, query, back, *rest):
    out = [far(BLOCK, BF16)] * 4 + [far(LAST, BF16), far(BLOCK, BF16)]
    scratch = [pltpu.VMEM(m.shape, BF16) for m in rest[1:3]]
    scratch += [pltpu.VMEM(FREQ, BF16), pltpu.VMEM(FREQ, BF16), MID, MID]
    scratch += [pltpu.VMEM(BLOCK, BF16)] * 2
    scratch += [pltpu.VMEM((SPLIT, *BLOCK), BF16), pltpu.VMEM(LAST, BF16)]
    scratch += [pltpu.VMEM((SPLIT, CHB, CHB), BF16), sems(4 + 2 * SPLIT + PANELS // GROUP)]
    specs = [SMEM] + [VMEM] * 9 + [HBM] * 4
    return call(middle_kernel, specs, out, scratch, 1 << 33, "middle", [HBM] * 6)(
        where, got, x, freq_x, rate, own_skip, *held, query, back, *rest
    )


def make_pair(own, two):
    scratch = [pltpu.VMEM(BLOCK, BF16), pltpu.SemaphoreType.DMA]
    return call(pair_kernel, [HBM, VMEM], here(BLOCK, F32), scratch, 1 << 36, "pair")(own, two)


def make_finish(got, key_in, value_in, pair, one, three):
    out = [shape(BLOCK, BF16)] * 3 + [shape(BLOCK, F32), shape((CHB // PANEL, PANEL), F32)]
    scratch = [pltpu.VMEM(BLOCK, BF16)] * 3 + [pltpu.VMEM(BLOCK, F32), sems(4 * CHB // CHUNK)]
    specs = [HBM] * 4 + [VMEM]
    return call(finish_kernel, [VMEM] * 6, out, scratch, 1 << 20, "finish", specs)(
        got, key_in, value_in, pair, one, three
    )


def shifted(value, step):
    return lax.ppermute(value, "ch", [(i, (i + step) % SPLIT) for i in range(SPLIT)])


def exchange(value):
    return lax.all_to_all(value, "ctx", 0, 0)


def local(query, key_in, value_in, filter_raw, decay, skip, out_weight, cotangent):
    mats = [jnp.asarray(m) for m in tables()]
    where = jnp.stack([lax.axis_index("ctx"), lax.axis_index("ch")]).astype(jnp.int32)
    lines = (CHB // PANEL, PANEL)
    cots = [shifted(cotangent, s) for s in (1, 2, 3)]
    x = exchange(make_product(key_in, value_in))
    lined = (decay.reshape(lines), skip.reshape(lines))
    freq_filter, rate, own_skip, *held, turned, share = make_filter(
        where, filter_raw, *lined, *mats[:2], query, cotangent, out_weight
    )
    send, freq_x, back = make_forward(
        where, x, own_skip, held, turned, share, out_weight, cots, freq_filter, mats[2:]
    )
    got = exchange(send)
    own, one, two, three, last, d_query = make_middle(
        where, got, x, freq_x, rate, own_skip, held, turned, back, freq_filter, *mats[2:], out_weight
    )
    last = exchange(last)
    pair = make_pair(own, shifted(two, 2))
    mixed, d_key, d_value, filter_grad, skip_grad = make_finish(
        last, key_in, value_in, pair, shifted(one, 1), shifted(three, 3)
    )
    return (mixed, d_query, d_key, d_value, filter_grad, skip_grad.reshape(CHB))


def solution(mesh):
    in_specs = (
        P("ctx", "ch"),
        P("ctx", "ch"),
        P("ctx", "ch"),
        P(None, "ch"),
        P("ch"),
        P("ch"),
        P("ch", None),
        P("ctx", "ch"),
    )
    out_specs = (
        P("ctx", "ch"),
        P("ctx", "ch"),
        P("ctx", "ch"),
        P("ctx", "ch"),
        P("ctx", "ch"),
        P("ch"),
    )
    return jax.shard_map(local, mesh=mesh, in_specs=in_specs, out_specs=out_specs, check_vma=False)
```
